512 devices in a mesh: pipe: 32 (over x_lo, z), tensor: 4 (over y), dp: 4 (over x_hi, core).
Axes of the slice: x: 4 (x_hi: 2, x_lo: 2; x = x_hi * 2 + x_lo), y: 4, z: 16, core: 2. Of those that a mesh axis runs over, the one named last changes fastest.
Arguments:
- grad_in: bfloat16 [32, 4, 128, 8192], P('pipe', 'dp', 'tensor'), may hold values from -6 to 6
- saved_x: bfloat16 [32, 4, 3, 128, 8192], P('pipe', 'dp', None, None, 'tensor'), may hold values from -6 to 6
- saved_z: bfloat16 [32, 4, 3, 128, 8192], P('pipe', 'dp', None, None, 'tensor'), may hold values from -6 to 6
- saved_dt: float32 [32, 4, 3, 128, 128], P('pipe', 'dp', None, None, 'tensor'), may hold values from 0.5 to 1.5
- saved_b: bfloat16 [32, 4, 3, 128, 8, 128], P('pipe', 'dp', None, None, 'tensor'), may hold values from -0.5 to 0.5
- saved_c: bfloat16 [32, 4, 3, 128, 8, 128], P('pipe', 'dp', None, None, 'tensor'), may hold values from -6 to 6
- a_log: float32 [32, 2, 128], P('pipe', None, 'tensor'), may hold values from -6.2 to -3
- dskip: float32 [32, 2, 128], P('pipe', None, 'tensor'), may hold values from 0.5 to 1.5
- gain: float32 [32, 2, 8192], P('pipe', None, 'tensor'), may hold values from 0.5 to 1.5
- block_table: int32 [2, 32, 4], P(None, 'pipe', 'dp'), may hold values from 0 to 1
- entry_table: int32 [2, 32, 4], P(None, 'pipe', 'dp'), may hold values from 0 to 2
Outputs:
- grad_out: bfloat16 [32, 4, 128, 8192], P('pipe', 'dp', 'tensor')
- grad_alog: float32 [32, 2, 128], P('pipe', None, ('tensor', 'dp'))
- grad_dskip: float32 [32, 2, 128], P('pipe', None, ('tensor', 'dp'))
- grad_gain: float32 [32, 2, 8192], P('pipe', None, ('tensor', 'dp'))
The draws below stay inside these ranges and needn't reach their ends.
All inputs are finite; a program needn't handle non-finite values.
Results may differ from the reference program's by a relative error of at most 0.023.
Values may be sent and summed in bfloat16 or wider, within the bound.
No kernel may reach another device: no remote copies, remote signals or barrier semaphores. Data moves between devices by JAX's collectives and lax.ppermute only.
A program may use at most 64 MiB of HBM per device.

```python
from functools import partial
import jax
import jax.numpy as jnp
from jax import lax

HEADS = 128
HEAD_DIM = 64
GROUPS = 8
STATE = 128
SEQ = 128
ENTRIES = 3
TICKS = 2
BLOCKS = 2
SECTIONS = 32
REPLICAS = 4


def touch_ends(drawn, own_key, least, largest):
    longest = drawn.shape.index(max(drawn.shape))
    spots = []
    for shift in (0, 1):
        where = [jax.random.randint(jax.random.fold_in(own_key, axis), (), 0, length) for axis, length in enumerate(drawn.shape)]
        where[longest] = (where[longest] + shift) % drawn.shape[longest]
        spots.append(tuple(where))
    return drawn.at[spots[0]].set(least).at[spots[1]].set(largest)


def steps_of(rng, extent, cuts, low, top_value):
    factor_of, own = 1.0, jax.random.fold_in(rng, 6)
    for position, shards_of in cuts:
        heights = jnp.exp(jax.random.uniform(jax.random.fold_in(own, position), (shards_of,), jnp.float32, low / len(cuts), top_value / len(cuts)))
        factor_of = factor_of * jnp.repeat(heights, extent[position] // shards_of).reshape([-1 if axis == position else 1 for axis in range(len(extent))])
    return factor_of


def noise(rng, shape, spread, bound, pieces=(), kind=jnp.bfloat16):
    drawn = jax.random.normal(rng, shape, jnp.float32) * spread
    if len(pieces) > 0:
        drawn = steps_of(rng, shape, pieces, -0.22, 0.18) * drawn
    return jnp.clip(drawn, min=-bound, max=bound).astype(kind)


def setup_inputs(seed: int = 0) -> dict:
    streams_of = jax.random.split(jax.random.key(seed), 12)
    grad_in = noise(streams_of[0], (SECTIONS, REPLICAS, SEQ, HEADS * HEAD_DIM), 1.0, 6.0, ((0, 32), (1, 4), (2, 4)))
    saved_x = noise(streams_of[1], (SECTIONS, REPLICAS, ENTRIES, SEQ, HEADS * HEAD_DIM), 1.0, 6.0, ((0, 32), (1, 4), (4, 4)))
    saved_z = noise(streams_of[2], (SECTIONS, REPLICAS, ENTRIES, SEQ, HEADS * HEAD_DIM), 1.0, 6.0, ((0, 32), (1, 4), (4, 4)))
    saved_dt = jnp.clip(0.5 + 1.0 * jax.random.uniform(streams_of[3], (SECTIONS, REPLICAS, ENTRIES, SEQ, HEADS), jnp.float32) ** steps_of(streams_of[3], (SECTIONS, REPLICAS, ENTRIES, SEQ, HEADS), ((0, 32), (1, 4), (4, 4)), -0.2, 0.2), 0.5, 1.5)
    saved_b = noise(streams_of[4], (SECTIONS, REPLICAS, ENTRIES, SEQ, GROUPS, STATE), STATE ** -0.5, 0.5, ((0, 32), (1, 4), (4, 4)))
    saved_c = noise(streams_of[5], (SECTIONS, REPLICAS, ENTRIES, SEQ, GROUPS, STATE), 1.0, 6.0, ((0, 32), (1, 4), (4, 4)))
    a_log = jnp.clip(-6.2 + 3.1999998 * jax.random.uniform(streams_of[6], (SECTIONS, BLOCKS, HEADS), jnp.float32) ** steps_of(streams_of[6], (SECTIONS, BLOCKS, HEADS), ((0, 32), (2, 4)), -0.2, 0.2), -6.2, -3.0)
    dskip = jnp.clip(0.5 + 1.0 * jax.random.uniform(streams_of[7], (SECTIONS, BLOCKS, HEADS), jnp.float32) ** steps_of(streams_of[7], (SECTIONS, BLOCKS, HEADS), ((0, 32), (2, 4)), -0.2, 0.2), 0.5, 1.5)
    gain = jnp.clip(1.0 + 0.1 * jax.random.normal(streams_of[8], (SECTIONS, BLOCKS, HEADS * HEAD_DIM), jnp.float32), 0.5, 1.5)
    block_table = touch_ends(jax.random.randint(streams_of[9], (TICKS, SECTIONS, REPLICAS), 0, BLOCKS), jax.random.fold_in(streams_of[9], 1), 0, BLOCKS - 1).astype(jnp.int32)
    entry_table = touch_ends(jax.random.randint(streams_of[10], (TICKS, SECTIONS, REPLICAS), 0, ENTRIES), jax.random.fold_in(streams_of[10], 1), 0, ENTRIES - 1).astype(jnp.int32)
    return {"grad_in": grad_in, "saved_x": saved_x, "saved_z": saved_z, "saved_dt": saved_dt, "saved_b": saved_b, "saved_c": saved_c, "a_log": a_log, "dskip": dskip, "gain": gain, "block_table": block_table, "entry_table": entry_table}


eps = 1e-05

def mix_terms(zf, dtv, bmat, cmat, u, a_log, dskip):
    seq = u.shape[0]
    heads = a_log.shape[0]
    width = u.shape[1] // heads
    groups = bmat.shape[1]
    ux = u.reshape(seq, heads, width)
    cum = -jnp.cumsum(dtv * jnp.exp(a_log)[None, :], axis=0)
    pos = jnp.arange(seq, dtype=jnp.int32)
    causal = (pos[:, None] >= pos[None, :])[None]
    diff = cum.T[:, :, None] - cum.T[:, None, :]
    decay = jnp.where(causal, jnp.exp(jnp.where(causal, diff, 0.0)), 0.0)
    scores = jnp.einsum('tgn,sgn->gts', cmat, bmat)
    scores = jnp.repeat(scores, heads // groups, axis=0)
    drive = ux * dtv[:, :, None]
    y = jnp.einsum('hts,shp->thp', scores * decay, drive) + dskip[None, :, None] * ux
    return y.reshape(seq, heads * width) * jax.nn.silu(zf)

def block_out(zf, dtv, bmat, cmat, u, a_log, dskip, gain):
    gated = mix_terms(zf, dtv, bmat, cmat, u, a_log, dskip)
    seq = gated.shape[0]
    chan = gated.shape[1]
    groups = bmat.shape[1]
    grouped = gated.reshape(seq, groups, chan // groups)
    mean_sq = lax.optimization_barrier(jnp.mean(grouped * grouped, axis=2))
    normed = grouped * lax.rsqrt(mean_sq + eps)[:, :, None]
    return normed.reshape(seq, chan) * gain[None, :]

def reference(grad_in, saved_x, saved_z, saved_dt, saved_b, saved_c, a_log, dskip, gain, block_table, entry_table):
    sections = grad_in.shape[0]
    replicas = grad_in.shape[1]
    current = grad_in
    acc_al = jnp.zeros((sections, replicas, BLOCKS, HEADS), jnp.float32)
    acc_ds = jnp.zeros((sections, replicas, BLOCKS, HEADS), jnp.float32)
    acc_gn = jnp.zeros((sections, replicas, BLOCKS, HEADS * HEAD_DIM), jnp.float32)
    result = current
    for tick in range(TICKS):
        blocks_now = block_table[tick]
        entries_now = entry_table[tick]

        def item(index):
            section = index // replicas
            rep = index % replicas
            block = blocks_now[section, rep]
            entry = entries_now[section, rep]
            u = saved_x[section, rep, entry].astype(jnp.float32)
            zf = saved_z[section, rep, entry].astype(jnp.float32)
            dtv = saved_dt[section, rep, entry]
            bmat = saved_b[section, rep, entry].astype(jnp.float32)
            cmat = saved_c[section, rep, entry].astype(jnp.float32)
            g = current[section, rep].astype(jnp.float32)
            func = partial(block_out, zf, dtv, bmat, cmat)
            _, pull = jax.vjp(func, u, a_log[section, block], dskip[section, block], gain[section, block])
            du, dal, dds, dgn = pull(g)
            return ((g + du).astype(jnp.bfloat16), dal, dds, dgn)
        dx, dal, dds, dgn = lax.map(item, jnp.arange(sections * replicas, dtype=jnp.int32))
        dx = dx.reshape(sections, replicas, SEQ, HEADS * HEAD_DIM)
        onehot = (jnp.arange(BLOCKS, dtype=jnp.int32)[None, None, :] == blocks_now[:, :, None]).astype(jnp.float32)
        acc_al = acc_al + onehot[..., None] * dal.reshape(sections, replicas, 1, HEADS)
        acc_ds = acc_ds + onehot[..., None] * dds.reshape(sections, replicas, 1, HEADS)
        acc_gn = acc_gn + onehot[..., None] * dgn.reshape(sections, replicas, 1, HEADS * HEAD_DIM)
        result = dx
        current = jnp.roll(dx, -1, axis=0)
    return (result, lax.optimization_barrier(jnp.sum(acc_al, axis=1)), lax.optimization_barrier(jnp.sum(acc_ds, axis=1)), lax.optimization_barrier(jnp.sum(acc_gn, axis=1)))
```

```python
from functools import partial

import jax
import jax.numpy as jnp
from jax import lax
from jax.experimental import pallas as pl
from jax.experimental.pallas import tpu as pltpu
from jax.sharding import PartitionSpec as P

eps = 1e-05
f32 = jnp.float32
bf16 = jnp.bfloat16
LANES = 128


def passed_along(block, axis, distance):
    devices = range(lax.axis_size(axis))
    route = [((i - distance) % len(devices), i) for i in devices]
    return lax.ppermute(block, axis, route)


def spread(columns, first, width):
    rows = columns.shape[0]
    lane = lax.broadcasted_iota(jnp.int32, (rows, LANES), 1)
    left = jnp.broadcast_to(columns[:, first : first + 1], (rows, LANES))
    right = jnp.broadcast_to(columns[:, first + 1 : first + 2], (rows, LANES))
    return jnp.where(lane < width, left, right)


def thirds(value):
    high = value.astype(bf16)
    rest = value - high.astype(f32)
    middle = rest.astype(bf16)
    return high, middle, (rest - middle.astype(f32)).astype(bf16)


def of_block(ref, block, here=slice(None)):
    rows = ref[0, :, here]
    row = rows[0:1]
    for other in range(1, rows.shape[0]):
        row = jnp.where(block == other, rows[other : other + 1], row)
    return row


def forward(
    tick,
    block_ref,
    entry_ref,
    x_ref,
    z_ref,
    dt_ref,
    b_ref,
    c_ref,
    alog_ref,
    dskip_ref,
    gain_ref,
    a1_ref,
    b1_ref,
    n_ref,
    e1_ref,
    wx_ref,
    yc_ref,
    wc_ref,
    st_ref,
    drive_ref,
    y_ref,
):
    block = block_ref[tick, 0, 0]
    seq, chan = n_ref.shape
    groups = st_ref.shape[0]
    heads = dt_ref.shape[-1]
    width = chan // heads
    per_group = chan // groups
    tiles = per_group // LANES
    row = lax.broadcasted_iota(jnp.int32, (seq, seq), 0)
    col = lax.broadcasted_iota(jnp.int32, (seq, seq), 1)
    dt = dt_ref[0, 0, 0]
    rate = jnp.exp(of_block(alog_ref, block))
    lower = (row >= col).astype(bf16)
    cum = -sum(jnp.dot(lower, part, preferred_element_type=f32) for part in thirds(dt * rate))
    grow = jnp.exp(-cum)
    fall = jnp.exp(cum)
    weight = grow * dt
    for group in range(groups):
        bmat = b_ref[0, 0, 0, :, group, :]
        cmat = c_ref[0, 0, 0, :, group, :]
        st = lax.dot_general(bmat, cmat, (((1,), (1,)), ((), ())), preferred_element_type=f32)
        st_ref[group] = jnp.where(row <= col, st, 0.0).astype(bf16)
        scores = lax.dot_general(cmat, bmat, (((1,), (1,)), ((), ())), preferred_element_type=f32)
        scores = jnp.where(row >= col, scores, 0.0).astype(bf16)
        for tile in range(tiles):
            here = pl.ds(group * per_group + tile * LANES, LANES)
            head = (group * per_group + tile * LANES) // width
            wx = spread(weight, head, width)
            wx_ref[:, here] = wx
            drive = (wx * x_ref[0, 0, 0, :, here].astype(f32)).astype(bf16)
            drive_ref[:, pl.ds(tile * LANES, LANES)] = drive
            wc_ref[:, here] = spread(cum, head, width) * drive.astype(f32)
        y_ref[...] = jnp.dot(scores, drive_ref[...], preferred_element_type=f32)
        total = jnp.zeros((seq, LANES), f32)
        for tile in range(tiles):
            here = pl.ds(group * per_group + tile * LANES, LANES)
            head = (group * per_group + tile * LANES) // width
            mixed = y_ref[:, pl.ds(tile * LANES, LANES)]
            yc_ref[:, here] = spread(cum, head, width) * mixed
            e1_ref[:, here] = spread(grow, head, width)
            ec = spread(fall, head, width)
            skip = spread(of_block(dskip_ref, block), head, width)
            z = z_ref[0, 0, 0, :, here].astype(f32)
            gate = z * jax.nn.sigmoid(z)
            gated = (ec * mixed + skip * x_ref[0, 0, 0, :, here].astype(f32)) * gate
            total = total + gated * gated
            n_ref[:, here] = gated
            a1_ref[:, here] = ec * gate
        scale = lax.rsqrt(jnp.sum(total, axis=1, keepdims=True) * (1.0 / per_group) + eps)
        for tile in range(tiles):
            here = pl.ds(group * per_group + tile * LANES, LANES)
            normed = n_ref[:, here] * scale
            n_ref[:, here] = normed
            slope = a1_ref[:, here] * scale
            a1_ref[:, here] = slope * of_block(gain_ref, block, here)
            b1_ref[:, here] = slope * normed


def backward(
    tick,
    block_ref,
    entry_ref,
    x_ref,
    dskip_ref,
    gain_ref,
    g_ref,
    a1_ref,
    b1_ref,
    n_ref,
    e1_ref,
    wx_ref,
    yc_ref,
    wc_ref,
    st_ref,
    dx_ref,
    rows_ref,
    v_ref,
    q_ref,
    part_ref,
):
    block = block_ref[tick, 0, 0]
    seq, chan = n_ref.shape
    groups = st_ref.shape[0]
    heads = dskip_ref.shape[-1]
    width = chan // heads
    per_group = chan // groups
    tiles = per_group // LANES
    for group in range(groups):
        total = jnp.zeros((seq, LANES), f32)
        for tile in range(tiles):
            here = pl.ds(group * per_group + tile * LANES, LANES)
            gn = g_ref[:, here].astype(f32) * n_ref[:, here]
            rows_ref[0:1, here] = jnp.sum(gn, axis=0, keepdims=True)
            total = total + gn * of_block(gain_ref, block, here)
        mean = jnp.sum(total, axis=1, keepdims=True) * (1.0 / per_group)
        for tile in range(tiles):
            here = pl.ds(group * per_group + tile * LANES, LANES)
            there = pl.ds(tile * LANES, LANES)
            head = (group * per_group + tile * LANES) // width
            g = g_ref[:, here].astype(f32)
            v = a1_ref[:, here] * g - b1_ref[:, here] * mean
            vb = v.astype(bf16)
            v_ref[:, there] = vb
            dy = e1_ref[:, here] * v
            skip = spread(of_block(dskip_ref, block), head, width)
            part_ref[:, there] = g + skip * dy
            rows_ref[2:3, here] = jnp.sum(dy * x_ref[0, 0, 0, :, here].astype(f32), axis=0, keepdims=True)
            rows_ref[1:2, here] = jnp.sum(vb.astype(f32) * yc_ref[:, here], axis=0, keepdims=True)
        q_ref[...] = jnp.dot(st_ref[group], v_ref[...], preferred_element_type=f32)
        for tile in range(tiles):
            here = pl.ds(group * per_group + tile * LANES, LANES)
            there = pl.ds(tile * LANES, LANES)
            q = q_ref[:, there]
            dx_ref[:, here] = (part_ref[:, there] + wx_ref[:, here] * q).astype(bf16)
            rows_ref[1:2, here] -= jnp.sum(wc_ref[:, here] * q, axis=0, keepdims=True)


def pack(block_ref, first_ref, second_ref, packet_ref):
    parts, _, share = packet_ref.shape
    packet_ref[...] = jnp.zeros(packet_ref.shape, f32)
    for block in range(2):
        for kind in range(3):
            row = jnp.where(block_ref[0, 0, 0] == block, first_ref[kind : kind + 1, :], 0.0)
            row = row + jnp.where(block_ref[1, 0, 0] == block, second_ref[kind : kind + 1, :], 0.0)
            for part in range(parts):
                at = 2 * kind + block
                packet_ref[part, at : at + 1, :] = row[:, part * share : (part + 1) * share]


def unpack(packet_ref, alog_ref, dskip_ref, gain_ref):
    parts, _, share = packet_ref.shape
    total = packet_ref[0]
    for part in range(1, parts):
        total = total + packet_ref[part]
    gain_ref[0] = total[0:2]
    heads = alog_ref.shape[-1]
    lane = lax.broadcasted_iota(jnp.int32, (share, heads), 0)
    head = lax.broadcasted_iota(jnp.int32, (share, heads), 1)
    same = (lane // (share // heads) == head).astype(bf16)
    sums = sum(jnp.dot(part, same, preferred_element_type=f32) for part in thirds(total))
    alog_ref[0] = sums[2:4]
    dskip_ref[0] = sums[4:6]


def relay_out(x_ref, out_ref, sem):
    parts, _, share = out_ref.shape
    copies = [
        pltpu.make_async_copy(x_ref.at[0, 0, :, pl.ds(i * share, share)], out_ref.at[i], sem.at[i]) for i in range(parts)
    ]
    for copy in copies:
        copy.start()
    for copy in copies:
        copy.wait()


def relay_in(x_ref, out_ref, sem):
    parts, _, share = x_ref.shape
    copies = [
        pltpu.make_async_copy(x_ref.at[i], out_ref.at[0, 0, :, pl.ds(i * share, share)], sem.at[i]) for i in range(parts)
    ]
    for copy in copies:
        copy.start()
    for copy in copies:
        copy.wait()


MIB = 1 << 20
in_vmem = pl.BlockSpec(memory_space=pltpu.VMEM)
in_any = pl.BlockSpec(memory_space=pl.ANY)


def entry_spec(shape, tick):
    block = (1, 1, 1) + tuple(shape[3:])
    rest = (0,) * (len(shape) - 3)
    return pl.BlockSpec(block, lambda i, bt, et: (0, 0, et[tick, 0, 0]) + rest)


def whole(shape):
    zeros = (0,) * len(shape)
    return pl.BlockSpec(tuple(shape), lambda i, bt, et: zeros)


def run_forward(tick, block_table, entry_table, x, z, dt, b, c, alog, dskip, gain):
    seq, chan = x.shape[3:]
    groups = b.shape[4]
    arrays = [jax.ShapeDtypeStruct((seq, chan), f32)] * 7 + [jax.ShapeDtypeStruct((groups, seq, seq), bf16)]
    return pl.pallas_call(
        partial(forward, tick),
        grid_spec=pltpu.PrefetchScalarGridSpec(
            num_scalar_prefetch=2,
            grid=(1,),
            in_specs=[entry_spec(a.shape, tick) for a in (x, z, dt, b, c)] + [whole(a.shape) for a in (alog, dskip, gain)],
            out_specs=[whole(a.shape) for a in arrays],
            scratch_shapes=[pltpu.VMEM((seq, chan // groups), bf16), pltpu.VMEM((seq, chan // groups), f32)],
        ),
        out_shape=arrays,
        compiler_params=pltpu.CompilerParams(vmem_limit_bytes=32 * MIB),
        cost_estimate=pl.CostEstimate(flops=200 * 1000 * 1000, bytes_accessed=9 * MIB, transcendentals=seq * chan),
        name="forward",
    )(block_table, entry_table, x, z, dt, b, c, alog, dskip, gain)


def run_backward(tick, block_table, entry_table, x, dskip, gain, g, saved):
    seq, chan = x.shape[3:]
    groups = saved[-1].shape[0]
    outs = [jax.ShapeDtypeStruct((seq, chan), bf16), jax.ShapeDtypeStruct((3, chan), f32)]
    per_group = chan // groups
    return pl.pallas_call(
        partial(backward, tick),
        grid_spec=pltpu.PrefetchScalarGridSpec(
            num_scalar_prefetch=2,
            grid=(1,),
            in_specs=[entry_spec(x.shape, tick)] + [whole(a.shape) for a in (dskip, gain, g, *saved)],
            out_specs=[whole(a.shape) for a in outs],
            scratch_shapes=[
                pltpu.VMEM((seq, per_group), bf16),
                pltpu.VMEM((seq, per_group), f32),
                pltpu.VMEM((seq, per_group), f32),
            ],
        ),
        out_shape=outs,
        compiler_params=pltpu.CompilerParams(vmem_limit_bytes=32 * MIB),
        cost_estimate=pl.CostEstimate(flops=200 * 1000 * 1000, bytes_accessed=9 * MIB, transcendentals=0),
        name="backward",
    )(block_table, entry_table, x, dskip, gain, g, *saved)


def shards(
    grad_in,
    saved_x,
    saved_z,
    saved_dt,
    saved_b,
    saved_c,
    a_log,
    dskip,
    gain,
    block_table,
    entry_table,
):
    parts = lax.axis_size("tensor")
    replicas = lax.axis_size("dp")
    tokens, channels = grad_in.shape[2:]
    share = channels // parts
    seq = tokens * parts
    heads = a_log.shape[2]
    blocks = a_log.shape[1]
    tables = (block_table, entry_table)
    staged = pl.pallas_call(
        relay_out,
        in_specs=[in_any],
        out_specs=in_any,
        out_shape=jax.ShapeDtypeStruct((parts, tokens, share), bf16),
        scratch_shapes=[pltpu.SemaphoreType.DMA((parts,))],
        name="relay_out",
    )(grad_in)
    g = lax.all_to_all(staged, "tensor", split_axis=0, concat_axis=0, tiled=True).reshape(seq, share)
    saved = [
        run_forward(tick, *tables, saved_x, saved_z, saved_dt, saved_b, saved_c, a_log, dskip, gain) for tick in range(2)
    ]
    dx, rows0 = run_backward(0, *tables, saved_x, dskip, gain, g, saved[0])
    g = passed_along(dx, "pipe", -1)
    dx, rows1 = run_backward(1, *tables, saved_x, dskip, gain, g, saved[1])
    out = lax.all_to_all(dx.reshape(parts, tokens, share), "tensor", split_axis=0, concat_axis=0, tiled=True)
    packet = pl.pallas_call(
        pack,
        in_specs=[pl.BlockSpec(memory_space=pltpu.SMEM), in_vmem, in_vmem],
        out_specs=in_vmem,
        out_shape=jax.ShapeDtypeStruct((replicas, 8, share // replicas), f32),
        name="pack",
    )(block_table, rows0, rows1)
    packet = lax.all_to_all(packet, "dp", split_axis=0, concat_axis=0, tiled=True)
    grad_alog, grad_dskip, grad_gain = pl.pallas_call(
        unpack,
        in_specs=[in_vmem],
        out_specs=[in_vmem] * 3,
        out_shape=[
            jax.ShapeDtypeStruct((1, blocks, heads // replicas), f32),
            jax.ShapeDtypeStruct((1, blocks, heads // replicas), f32),
            jax.ShapeDtypeStruct((1, blocks, share // replicas), f32),
        ],
        name="unpack",
    )(packet)
    out = pl.pallas_call(
        relay_in,
        in_specs=[in_any],
        out_specs=in_any,
        out_shape=jax.ShapeDtypeStruct(grad_in.shape, bf16),
        scratch_shapes=[pltpu.SemaphoreType.DMA((parts,))],
        name="relay_in",
    )(out)
    return (out, grad_alog, grad_dskip, grad_gain)


def solution(mesh):
    placed = (
        P("pipe", "dp", "tensor", None),
        P("pipe", "dp", None, None, "tensor"),
        P("pipe", "dp", None, None, "tensor"),
        P("pipe", "dp", None, None, "tensor"),
        P("pipe", "dp", None, None, "tensor", None),
        P("pipe", "dp", None, None, "tensor", None),
        P("pipe", None, "tensor"),
        P("pipe", None, "tensor"),
        P("pipe", None, "tensor"),
        P(None, "pipe", "dp"),
        P(None, "pipe", "dp"),
    )
    return jax.shard_map(
        shards,
        mesh=mesh,
        in_specs=placed,
        out_specs=(
            P("pipe", "dp", "tensor", None),
            P("pipe", None, ("tensor", "dp")),
            P("pipe", None, ("tensor", "dp")),
            P("pipe", None, ("tensor", "dp")),
        ),
        check_vma=False,
    )
```

```python
from functools import partial

import jax
import jax.numpy as jnp
from jax import lax
from jax.experimental import pallas as pl
from jax.experimental.pallas import tpu as pltpu
from jax.sharding import PartitionSpec as P

eps = 1e-05
f32 = jnp.float32
bf16 = jnp.bfloat16
LANES = 128


def passed_along(block, axis, distance):
    devices = range(lax.axis_size(axis))
    route = [((i - distance) % len(devices), i) for i in devices]
    return lax.ppermute(block, axis, route)


def thirds(value):
    high = value.astype(bf16)
    rest = value - high.astype(f32)
    middle = rest.astype(bf16)
    return high, middle, (rest - middle.astype(f32)).astype(bf16)


def of_block(ref, block, here=slice(None)):
    rows = ref[0, :, here]
    row = rows[0:1]
    for other in range(1, rows.shape[0]):
        row = jnp.where(block == other, rows[other : other + 1], row)
    return row


def spread_map(heads, width):
    head = lax.broadcasted_iota(jnp.int32, (3 * heads, heads * width), 0) % heads
    lane = lax.broadcasted_iota(jnp.int32, (3 * heads, heads * width), 1)
    return (lane // width == head).astype(bf16)


def spread(values, one_hot):
    return jnp.dot(jnp.concatenate(thirds(values), axis=1), one_hot, preferred_element_type=f32)


def halves(value):
    high = value.astype(bf16)
    return high, (value - high.astype(f32)).astype(bf16)


def forward(
    tick,
    block_ref,
    entry_ref,
    x_hbm,
    z_hbm,
    dt_hbm,
    b_hbm,
    c_hbm,
    alog_ref,
    dskip_ref,
    gain_ref,
    x_ref,
    slope_ref,
    normed_ref,
    scores_ref,
    heads_ref,
    rows_ref,
    z_ref,
    dt_ref,
    b_ref,
    c_ref,
    drive_ref,
    wx_ref,
    ec_ref,
    y_ref,
    gated_ref,
    gate_ref,
    sem,
):
    block = block_ref[tick]
    entry = entry_ref[tick]
    moves = [
        pltpu.make_async_copy(src.at[0, 0, entry], dst, sem.at[i])
        for i, (src, dst) in enumerate(
            ((dt_hbm, dt_ref), (b_hbm, b_ref), (c_hbm, c_ref), (x_hbm, x_ref), (z_hbm, z_ref))
        )
    ]
    for move in moves:
        move.start()
    seq, chan = normed_ref.shape
    groups = scores_ref.shape[0]
    heads = dt_ref.shape[0]
    width = chan // heads
    per_group = chan // groups
    held = heads // groups
    tiles = per_group // LANES
    row = lax.broadcasted_iota(jnp.int32, (seq, seq), 0)
    col = lax.broadcasted_iota(jnp.int32, (seq, seq), 1)
    rate = jnp.exp(of_block(alog_ref, block))
    one_hot = spread_map(held, width)
    rows_ref[0:1] = of_block(gain_ref, block)
    skips = jnp.broadcast_to(of_block(dskip_ref, block), (8, heads))
    for group in range(groups):
        mine = slice(group * held, (group + 1) * held)
        rows_ref[1:2, pl.ds(group * per_group, per_group)] = spread(skips[:, mine], one_hot)[0:1]
    moves[0].wait()
    lower = (row >= col).astype(bf16)
    same = (row == col).astype(bf16)
    taken = jnp.concatenate([jnp.concatenate([lower] * 3, axis=1), jnp.concatenate([same] * 3, axis=1)], axis=0)
    steps = jnp.concatenate(thirds(dt_ref[...]), axis=1)
    steps = lax.dot_general(taken, steps, (((1,), (1,)), ((), ())), preferred_element_type=f32)
    cum = -steps[0:seq] * rate
    grow = jnp.exp(-cum)
    fall = jnp.exp(cum)
    weight = grow * steps[seq:]
    heads_ref[:, 0:heads] = cum
    heads_ref[:, heads : 2 * heads] = grow
    heads_ref[:, 2 * heads : 3 * heads] = weight
    for group in range(groups):
        mine = slice(group * held, (group + 1) * held)
        both = spread(jnp.concatenate([weight[:, mine], fall[:, mine]], axis=0), one_hot)
        wx_ref[group] = both[0:seq]
        ec_ref[group] = both[seq:]
    moves[1].wait()
    moves[2].wait()
    mixers = []
    for group in range(groups):
        bmat = b_ref[:, group, :]
        cmat = c_ref[:, group, :]
        st = lax.dot_general(bmat, cmat, (((1,), (1,)), ((), ())), preferred_element_type=f32)
        scores_ref[group, 1], scores_ref[group, 2] = halves(jnp.where(row <= col, st, 0.0))
        scores = lax.dot_general(cmat, bmat, (((1,), (1,)), ((), ())), preferred_element_type=f32)
        high, low = halves(jnp.where(row >= col, scores, 0.0))
        scores_ref[group, 0] = high
        mixers.append(jnp.concatenate([high, high, low], axis=1))
    moves[3].wait()
    for group in range(groups):
        for tile in range(tiles):
            here = pl.ds(group * per_group + tile * LANES, LANES)
            there = pl.ds(tile * LANES, LANES)
            high, low = halves(wx_ref[group, :, there] * x_ref[:, here].astype(f32))
            drive_ref[group, 0:seq, there] = high
            drive_ref[group, seq : 2 * seq, there] = low
            drive_ref[group, 2 * seq :, there] = high
        y_ref[group] = jnp.dot(mixers[group], drive_ref[group], preferred_element_type=f32)
    moves[4].wait()
    for group in range(groups):
        total = jnp.zeros((seq, LANES), f32)
        for tile in range(tiles):
            here = pl.ds(group * per_group + tile * LANES, LANES)
            there = pl.ds(tile * LANES, LANES)
            ec = ec_ref[group, :, there]
            z = z_ref[:, here].astype(f32)
            gate = z * jax.nn.sigmoid(z)
            gated = (ec * y_ref[group, :, there] + rows_ref[1:2, here] * x_ref[:, here].astype(f32)) * gate
            total = total + gated * gated
            gated_ref[group, :, there] = gated
            gate_ref[group, :, there] = ec * gate
        scale = lax.rsqrt(jnp.sum(total, axis=1, keepdims=True) * (1.0 / per_group) + eps)
        for tile in range(tiles):
            here = pl.ds(group * per_group + tile * LANES, LANES)
            there = pl.ds(tile * LANES, LANES)
            normed_ref[:, here] = (gated_ref[group, :, there] * scale).astype(bf16)
            slope_ref[:, here] = gate_ref[group, :, there] * scale


def backward(g_ref, x_ref, slope_ref, normed_ref, scores_ref, heads_ref, rows_ref, scratch, dx_ref, want_rows):
    drive_ref, v_ref, q_ref, y_ref, part_ref, wide_ref = scratch
    seq, chan = normed_ref.shape
    groups = scores_ref.shape[0]
    heads = heads_ref.shape[1] // 3
    per_group = chan // groups
    held = heads // groups
    width = per_group // held
    tiles = per_group // LANES
    one_hot = spread_map(held, width)
    found = [[], [], []]
    means = []
    for group in range(groups):
        total = jnp.zeros((seq, LANES), f32)
        for tile in range(tiles):
            here = pl.ds(group * per_group + tile * LANES, LANES)
            gn = g_ref[:, here].astype(f32) * normed_ref[:, here].astype(f32)
            total = total + gn * rows_ref[0:1, here]
            if want_rows:
                found[0].append(jnp.sum(gn, axis=0, keepdims=True))
        means.append(jnp.sum(total, axis=1, keepdims=True) * (1.0 / per_group))
        kinds = range(3) if want_rows else range(1, 3)
        factors = [heads_ref[:, kind * heads + group * held : kind * heads + (group + 1) * held] for kind in kinds]
        wide_ref[group, kinds[0] * seq :] = spread(jnp.concatenate(factors, axis=0), one_hot)
    for group in range(groups):
        for tile in range(tiles):
            here = pl.ds(group * per_group + tile * LANES, LANES)
            there = pl.ds(tile * LANES, LANES)
            g = g_ref[:, here].astype(f32)
            v = slope_ref[:, here] * (g * rows_ref[0:1, here] - normed_ref[:, here].astype(f32) * means[group])
            high = v.astype(bf16)
            v_ref[group, 0:seq, there] = high
            if not want_rows:
                v_ref[group, seq : 2 * seq, there] = (v - high.astype(f32)).astype(bf16)
                v_ref[group, 2 * seq :, there] = high
            dy = wide_ref[group, seq : 2 * seq, there] * v
            if dx_ref is not None:
                part_ref[group, :, there] = g + rows_ref[1:2, here] * dy
            if want_rows:
                x = x_ref[:, here].astype(f32)
                found[1].append(jnp.sum(dy * x, axis=0, keepdims=True))
                drive_ref[group, :, there] = (wide_ref[group, 2 * seq :, there] * x).astype(bf16)
        if want_rows:
            q_ref[group] = jnp.dot(scores_ref[group, 1], v_ref[group, 0:seq], preferred_element_type=f32)
            y_ref[group] = jnp.dot(scores_ref[group, 0], drive_ref[group], preferred_element_type=f32)
        else:
            high = scores_ref[group, 1]
            mixer = jnp.concatenate([high, high, scores_ref[group, 2]], axis=1)
            q_ref[group] = jnp.dot(mixer, v_ref[group], preferred_element_type=f32)
    for group in range(groups):
        for tile in range(tiles):
            here = pl.ds(group * per_group + tile * LANES, LANES)
            there = pl.ds(tile * LANES, LANES)
            q = q_ref[group, :, there]
            if dx_ref is not None:
                dx_ref[:, here] = (part_ref[group, :, there] + wide_ref[group, 2 * seq :, there] * q).astype(bf16)
            if want_rows:
                pull = v_ref[group, 0:seq, there].astype(f32) * y_ref[group, :, there] - drive_ref[group, :, there].astype(f32) * q
                found[2].append(jnp.sum(wide_ref[group, 0:seq, there] * pull, axis=0, keepdims=True))
    return [jnp.concatenate(row, axis=1) for row in found] if want_rows else None


def gather_heads(rows, width):
    lane = lax.broadcasted_iota(jnp.int32, (rows.shape[0], LANES), 1)
    sums = jnp.zeros((rows.shape[0], LANES), f32)
    for tile in range(rows.shape[1] // LANES):
        part = rows[:, tile * LANES : (tile + 1) * LANES]
        for side in range(LANES // width):
            mine = jnp.where(lane // width == side, part, 0.0)
            total = jnp.sum(mine, axis=1, keepdims=True)
            sums = jnp.where(lane == tile * (LANES // width) + side, total, sums)
    return sums


def place_rows(found, block, heads, out_ref, earlier_ref):
    gains, skips, logs = found
    share = out_ref.shape[1] - LANES
    parts = gains.shape[1] // share
    for other in range(2):
        row = jnp.where(block == other, gains, 0.0)
        for part in range(parts):
            at = other * parts + part
            piece = row[:, part * share : (part + 1) * share]
            if earlier_ref is not None:
                piece = piece + earlier_ref[at : at + 1, 0:share]
            out_ref[at : at + 1, 0:share] = piece
    sums = gather_heads(jnp.concatenate([skips, logs], axis=0), gains.shape[1] // heads)[:, 0:heads]
    sums = [jnp.where(block == other, sums[kind : kind + 1], 0.0) for kind in range(2) for other in range(2)]
    sums = jnp.concatenate(sums, axis=1)
    if earlier_ref is not None:
        sums = sums + earlier_ref[0:1, share:]
    out_ref[0:1, share:] = sums
    out_ref[1:, share:] = jnp.zeros((out_ref.shape[0] - 1, LANES), f32)


def backward_first(*refs):
    backward(*refs[:7], refs[8:], refs[7], False)


def rows_first(block_ref, *refs):
    heads = refs[5].shape[1] // 3
    place_rows(backward(*refs[:7], refs[8:], None, True), block_ref[0], heads, refs[7], None)


def backward_last(block_ref, earlier_ref, *refs):
    heads = refs[5].shape[1] // 3
    found = backward(*refs[:7], refs[9:], refs[7], True)
    place_rows(found, block_ref[1], heads, refs[8], earlier_ref)


def finish(me_ref, x_ref, gathered_ref, out_ref, alog_ref, dskip_ref, gain_ref, gone):
    parts, _, share = x_ref.shape
    outs = [
        pltpu.make_async_copy(x_ref.at[i], out_ref.at[0, 0, :, pl.ds(i * share, share)], gone.at[i]) for i in range(parts)
    ]
    for copy in outs:
        copy.start()
    me = me_ref[0]
    total = sum(gathered_ref[i] for i in range(gathered_ref.shape[0]))
    lanes = gain_ref.shape[2]
    replicas = total.shape[0] // 2
    held = alog_ref.shape[2]
    for block in range(2):
        row = total[block * replicas : block * replicas + 1, 0:lanes]
        skip, log = [total[0:1, lanes + (kind * 2 + block) * replicas * held :] for kind in range(2)]
        skips, logs = skip[:, 0:held], log[:, 0:held]
        for other in range(1, replicas):
            at = block * replicas + other
            row = jnp.where(me == other, total[at : at + 1, 0:lanes], row)
            skips = jnp.where(me == other, skip[:, other * held : (other + 1) * held], skips)
            logs = jnp.where(me == other, log[:, other * held : (other + 1) * held], logs)
        gain_ref[0, block : block + 1] = row
        dskip_ref[0, block : block + 1] = skips
        alog_ref[0, block : block + 1] = logs
    for copy in outs:
        copy.wait()


def relay_out(x_ref, out_ref, held_ref, came, gone):
    parts, _, share = out_ref.shape
    ins = [
        pltpu.make_async_copy(x_ref.at[0, 0, :, pl.ds(i * share, share)], held_ref.at[i], came.at[i]) for i in range(parts)
    ]
    outs = [pltpu.make_async_copy(held_ref.at[i], out_ref.at[i], gone.at[i]) for i in range(parts)]
    for copy in ins:
        copy.start()
    for first, second in zip(ins, outs):
        first.wait()
        second.start()
    for copy in outs:
        copy.wait()


in_vmem = pl.BlockSpec(memory_space=pltpu.VMEM)
in_smem = pl.BlockSpec(memory_space=pltpu.SMEM)
in_any = pl.BlockSpec(memory_space=pl.ANY)
MIB = 1 << 20


def sized(shape, dtype):
    return jax.ShapeDtypeStruct(tuple(shape), dtype)


def call(kernel, name, in_specs, out_specs, out_shape, scratch=(), grant=16, cost=1):
    return pl.pallas_call(
        kernel,
        in_specs=in_specs,
        out_specs=out_specs,
        out_shape=out_shape,
        scratch_shapes=list(scratch),
        compiler_params=pltpu.CompilerParams(vmem_limit_bytes=grant * MIB),
        cost_estimate=pl.CostEstimate(flops=1000, bytes_accessed=cost * 1000 * 1000, transcendentals=0),
        name=name,
    )


def run_forward(tick, block_table, entry_table, x, z, dt, b, c, alog, dskip, gain):
    seq, chan = x.shape[3:]
    groups = b.shape[4]
    heads = dt.shape[3]
    wide = (groups, seq, chan // groups)
    outs = [
        sized((seq, chan), bf16),
        sized((seq, chan), f32),
        sized((seq, chan), bf16),
        sized((groups, 3, seq, seq), bf16),
        sized((seq, 3 * heads), f32),
        sized((2, chan), f32),
    ]
    scratch = [
        pltpu.VMEM((seq, chan), bf16),
        pltpu.VMEM(dt.shape[3:], f32),
        pltpu.VMEM(b.shape[3:], bf16),
        pltpu.VMEM(c.shape[3:], bf16),
        pltpu.VMEM((groups, 3 * seq, chan // groups), bf16),
    ]
    scratch += [pltpu.VMEM(wide, f32)] * 5 + [pltpu.SemaphoreType.DMA((5,))]
    in_specs = [in_smem] * 2 + [in_any] * 5 + [in_vmem] * 3
    far = [pltpu.with_memory_space_constraint(a, pltpu.HBM) for a in (x, z, dt, b, c)]
    return call(partial(forward, tick), "forward", in_specs, [in_vmem] * 6, outs, scratch, 24, 12)(
        block_table, entry_table, *far, alog, dskip, gain
    )


def backward_scratch(seq, chan, groups):
    wide = (groups, seq, chan // groups)
    tall = (groups, 3 * seq, chan // groups)
    return [pltpu.VMEM(wide, bf16), pltpu.VMEM(tall, bf16)] + [pltpu.VMEM(wide, f32)] * 3 + [pltpu.VMEM(tall, f32)]


def shards(
    grad_in,
    saved_x,
    saved_z,
    saved_dt,
    saved_b,
    saved_c,
    a_log,
    dskip,
    gain,
    block_table,
    entry_table,
):
    parts = lax.axis_size("tensor")
    replicas = lax.axis_size("dp")
    tokens, channels = grad_in.shape[2:]
    share = channels // parts
    seq = tokens * parts
    heads = a_log.shape[2]
    blocks = a_log.shape[1]
    packet = sized((blocks * replicas, share // replicas + LANES), f32)
    block_table = block_table.reshape(-1)
    entry_table = entry_table.reshape(-1)
    steps = jnp.swapaxes(saved_dt, 3, 4)
    me = lax.axis_index("dp").reshape(1)
    staged = call(
        relay_out,
        "relay_out",
        [in_any],
        in_any,
        sized((parts, tokens, share), bf16),
        [pltpu.VMEM((parts, tokens, share), bf16)] + [pltpu.SemaphoreType.DMA((parts,))] * 2,
    )(pltpu.with_memory_space_constraint(grad_in, pltpu.HBM))
    g = lax.all_to_all(staged, "tensor", split_axis=0, concat_axis=0, tiled=True).reshape(seq, share)
    first, last = [
        run_forward(tick, block_table, entry_table, saved_x, saved_z, steps, saved_b, saved_c, a_log, dskip, gain)
        for tick in range(2)
    ]
    scratch = backward_scratch(seq, share, saved_b.shape[4])
    dx = call(backward_first, "backward_first", [in_vmem] * 7, in_vmem, sized((seq, share), bf16), scratch, 20, 6)(g, *first)
    earlier = call(rows_first, "rows_first", [in_smem] + [in_vmem] * 7, in_vmem, packet, scratch, 20, 6)(
        block_table, g, *first
    )
    g = passed_along(dx, "pipe", -1)
    dx, rows = call(
        backward_last,
        "backward_last",
        [in_smem] + [in_vmem] * 8,
        [in_vmem] * 2,
        [sized((seq, share), bf16), packet],
        scratch,
        20,
        6,
    )(block_table, earlier, g, *last)
    out = lax.all_to_all(dx.reshape(parts, tokens, share), "tensor", split_axis=0, concat_axis=0, tiled=True)
    rows = lax.all_gather(rows, "dp")
    out, grad_alog, grad_dskip, grad_gain = call(
        finish,
        "finish",
        [in_smem] + [in_vmem] * 2,
        [in_any] + [in_vmem] * 3,
        [
            sized(grad_in.shape, bf16),
            sized((1, blocks, heads // replicas), f32),
            sized((1, blocks, heads // replicas), f32),
            sized((1, blocks, share // replicas), f32),
        ],
        [pltpu.SemaphoreType.DMA((parts,))],
    )(me, out, rows)
    return (out, grad_alog, grad_dskip, grad_gain)


def solution(mesh):
    placed = (
        P("pipe", "dp", "tensor", None),
        P("pipe", "dp", None, None, "tensor"),
        P("pipe", "dp", None, None, "tensor"),
        P("pipe", "dp", None, None, "tensor"),
        P("pipe", "dp", None, None, "tensor", None),
        P("pipe", "dp", None, None, "tensor", None),
        P("pipe", None, "tensor"),
        P("pipe", None, "tensor"),
        P("pipe", None, "tensor"),
        P(None, "pipe", "dp"),
        P(None, "pipe", "dp"),
    )
    return jax.shard_map(
        shards,
        mesh=mesh,
        in_specs=placed,
        out_specs=(
            P("pipe", "dp", "tensor", None),
            P("pipe", None, ("tensor", "dp")),
            P("pipe", None, ("tensor", "dp")),
            P("pipe", None, ("tensor", "dp")),
        ),
        check_vma=False,
    )
```

```python
from functools import partial

import jax
import jax.numpy as jnp
from jax import lax
from jax.experimental import pallas as pl
from jax.experimental.pallas import tpu as pltpu
from jax.sharding import PartitionSpec as P

eps = 1e-05
f32 = jnp.float32
bf16 = jnp.bfloat16
LANES = 128
WIDTH = 64


def passed_along(block, axis, distance):
    devices = range(lax.axis_size(axis))
    route = [((i - distance) % len(devices), i) for i in devices]
    return lax.ppermute(block, axis, route)


def thirds(value):
    high = value.astype(bf16)
    rest = value - high.astype(f32)
    middle = rest.astype(bf16)
    return high, middle, (rest - middle.astype(f32)).astype(bf16)


def of_block(ref, block, here=slice(None)):
    rows = ref[0, :, here]
    row = rows[0:1]
    for other in range(1, rows.shape[0]):
        row = jnp.where(block == other, rows[other : other + 1], row)
    return row


def spread_map(heads, width):
    first = lax.broadcasted_iota(jnp.int32, (heads, heads * width), 0) * width
    lane = lax.broadcasted_iota(jnp.int32, (heads, heads * width), 1)
    one_hot = jnp.where((lane >= first) & (lane < first + width), 1.0, 0.0).astype(bf16)
    return jnp.concatenate([one_hot] * 3, axis=0)


def spread(values, one_hot):
    return jnp.dot(jnp.concatenate(thirds(values), axis=1), one_hot, preferred_element_type=f32)


def halves(value):
    high = value.astype(bf16)
    return high, (value - high.astype(f32)).astype(bf16)


def forward(
    tick,
    block_ref,
    entry_ref,
    x_hbm,
    z_hbm,
    dt_hbm,
    b_hbm,
    c_hbm,
    alog_ref,
    dskip_ref,
    gain_ref,
    slope_ref,
    normed_ref,
    scores_ref,
    rows_ref,
    *refs,
):
    if tick:
        wx_out, skips_ref, moved_ref, mixed_ref, driven_ref, wide_ref, x_ref, *refs = refs
    else:
        x_ref, heads_ref, *refs = refs
    z_ref, dt_ref, b_ref, c_ref, drive_ref, wx_ref, ec_ref, y_ref, gated_ref, gate_ref, sem = refs
    block = block_ref[tick]
    entry = entry_ref[tick]
    moves = [
        pltpu.make_async_copy(src.at[0, 0, entry], dst, sem.at[i])
        for i, (src, dst) in enumerate(
            ((dt_hbm, dt_ref), (b_hbm, b_ref), (c_hbm, c_ref), (x_hbm, x_ref), (z_hbm, z_ref))
        )
    ]
    for move in moves:
        move.start()
    seq, chan = normed_ref.shape
    groups = scores_ref.shape[0]
    heads = dt_ref.shape[0]
    width = chan // heads
    per_group = chan // groups
    held = heads // groups
    tiles = per_group // LANES
    row = lax.broadcasted_iota(jnp.int32, (seq, seq), 0)
    col = lax.broadcasted_iota(jnp.int32, (seq, seq), 1)
    rate = jnp.exp(of_block(alog_ref, block))
    one_hot = spread_map(held, width)
    rows_ref[0:1] = of_block(gain_ref, block)
    skips = jnp.broadcast_to(of_block(dskip_ref, block), (8, heads))
    for group in range(groups):
        mine = slice(group * held, (group + 1) * held)
        rows_ref[1:2, pl.ds(group * per_group, per_group)] = spread(skips[:, mine], one_hot)[0:1]
    moves[0].wait()
    lower = (row >= col).astype(bf16)
    same = (row == col).astype(bf16)
    taken = jnp.concatenate([jnp.concatenate([lower] * 3, axis=1), jnp.concatenate([same] * 3, axis=1)], axis=0)
    steps = jnp.concatenate(thirds(dt_ref[...]), axis=1)
    steps = lax.dot_general(taken, steps, (((1,), (1,)), ((), ())), preferred_element_type=f32)
    cum = -steps[0:seq] * rate
    grow = jnp.exp(-cum)
    fall = jnp.exp(cum)
    weight = grow * steps[seq:]
    if not tick:
        heads_ref[:, 0:heads] = cum
        heads_ref[:, heads : 2 * heads] = grow
        heads_ref[:, 2 * heads : 3 * heads] = weight
    for group in range(groups):
        mine = slice(group * held, (group + 1) * held)
        both = spread(jnp.concatenate([weight[:, mine], fall[:, mine]], axis=0), one_hot)
        wx_ref[group] = both[0:seq]
        ec_ref[group] = both[seq:]
        if tick:
            wide_ref[group] = spread(jnp.concatenate([grow[:, mine], cum[:, mine]], axis=0), one_hot)
    moves[1].wait()
    moves[2].wait()
    mixers = []
    for group in range(groups):
        bmat = b_ref[:, group, :]
        cmat = c_ref[:, group, :]
        st = lax.dot_general(bmat, cmat, (((1,), (1,)), ((), ())), preferred_element_type=f32)
        scores_ref[group, 1], scores_ref[group, 2] = halves(jnp.where(row <= col, st, 0.0))
        scores = lax.dot_general(cmat, bmat, (((1,), (1,)), ((), ())), preferred_element_type=f32)
        high, low = halves(jnp.where(row >= col, scores, 0.0))
        scores_ref[group, 0] = high
        mixers.append(jnp.concatenate([high, high, low], axis=1))
    moves[3].wait()
    for group in range(groups):
        for tile in range(tiles):
            here = pl.ds(group * per_group + tile * LANES, LANES)
            there = pl.ds(tile * LANES, LANES)
            x = x_ref[:, here].astype(f32)
            wx = wx_ref[group, :, there]
            high, low = halves(wx * x)
            if tick:
                wx_out[:, here] = wx
                grown = wide_ref[group, 0:seq, there]
                skips_ref[:, here] = grown * rows_ref[1:2, here]
                moved_ref[:, here] = grown * x
                driven_ref[:, here] = wide_ref[group, seq:, there] * high.astype(f32)
            drive_ref[group, 0:seq, there] = high
            drive_ref[group, seq : 2 * seq, there] = low
            drive_ref[group, 2 * seq :, there] = high
        if tick:
            y_ref[group] = jnp.dot(scores_ref[group, 0], drive_ref[group, 0:seq], preferred_element_type=f32)
            for tile in range(tiles):
                here = pl.ds(group * per_group + tile * LANES, LANES)
                there = pl.ds(tile * LANES, LANES)
                mixed_ref[:, here] = wide_ref[group, seq:, there] * y_ref[group, :, there]
        y_ref[group] = jnp.dot(mixers[group], drive_ref[group], preferred_element_type=f32)
    moves[4].wait()
    for group in range(groups):
        total = jnp.zeros((seq, LANES), f32)
        for tile in range(tiles):
            here = pl.ds(group * per_group + tile * LANES, LANES)
            there = pl.ds(tile * LANES, LANES)
            ec = ec_ref[group, :, there]
            z = z_ref[:, here].astype(f32)
            gate = z * jax.nn.sigmoid(z)
            gated = (ec * y_ref[group, :, there] + rows_ref[1:2, here] * x_ref[:, here].astype(f32)) * gate
            total = total + gated * gated
            gated_ref[group, :, there] = gated
            gate_ref[group, :, there] = ec * gate
        scale = lax.rsqrt(jnp.sum(total, axis=1, keepdims=True) * (1.0 / per_group) + eps)
        for tile in range(tiles):
            here = pl.ds(group * per_group + tile * LANES, LANES)
            there = pl.ds(tile * LANES, LANES)
            normed_ref[:, here] = (gated_ref[group, :, there] * scale).astype(bf16)
            slope_ref[:, here] = gate_ref[group, :, there] * scale


def backward(g_ref, slope_ref, normed_ref, scores_ref, rows_ref, x_ref, heads_ref, scratch, dx_ref, want_rows):
    drive_ref, v_ref, q_ref, y_ref, part_ref, wide_ref = scratch
    seq, chan = normed_ref.shape
    groups = scores_ref.shape[0]
    heads = heads_ref.shape[1] // 3
    per_group = chan // groups
    held = heads // groups
    width = per_group // held
    tiles = per_group // LANES
    one_hot = spread_map(held, width)
    found = [[], [], []]
    means = []
    for group in range(groups):
        total = jnp.zeros((seq, LANES), f32)
        for tile in range(tiles):
            here = pl.ds(group * per_group + tile * LANES, LANES)
            gn = g_ref[:, here].astype(f32) * normed_ref[:, here].astype(f32)
            total = total + gn * rows_ref[0:1, here]
            if want_rows:
                found[0].append(jnp.sum(gn, axis=0, keepdims=True))
        means.append(jnp.sum(total, axis=1, keepdims=True) * (1.0 / per_group))
        kinds = range(3) if want_rows else range(1, 3)
        factors = [heads_ref[:, kind * heads + group * held : kind * heads + (group + 1) * held] for kind in kinds]
        wide_ref[group, kinds[0] * seq :] = spread(jnp.concatenate(factors, axis=0), one_hot)
    for group in range(groups):
        for tile in range(tiles):
            here = pl.ds(group * per_group + tile * LANES, LANES)
            there = pl.ds(tile * LANES, LANES)
            g = g_ref[:, here].astype(f32)
            v = slope_ref[:, here] * (g * rows_ref[0:1, here] - normed_ref[:, here].astype(f32) * means[group])
            high = v.astype(bf16)
            v_ref[group, 0:seq, there] = high
            if not want_rows:
                v_ref[group, seq : 2 * seq, there] = (v - high.astype(f32)).astype(bf16)
                v_ref[group, 2 * seq :, there] = high
            dy = wide_ref[group, seq : 2 * seq, there] * v
            if dx_ref is not None:
                part_ref[group, :, there] = g + rows_ref[1:2, here] * dy
            if want_rows:
                x = x_ref[:, here].astype(f32)
                found[1].append(jnp.sum(dy * x, axis=0, keepdims=True))
                drive_ref[group, :, there] = (wide_ref[group, 2 * seq :, there] * x).astype(bf16)
        if want_rows:
            q_ref[group] = jnp.dot(scores_ref[group, 1], v_ref[group, 0:seq], preferred_element_type=f32)
            y_ref[group] = jnp.dot(scores_ref[group, 0], drive_ref[group], preferred_element_type=f32)
        else:
            high = scores_ref[group, 1]
            mixer = jnp.concatenate([high, high, scores_ref[group, 2]], axis=1)
            q_ref[group] = jnp.dot(mixer, v_ref[group], preferred_element_type=f32)
    for group in range(groups):
        for tile in range(tiles):
            here = pl.ds(group * per_group + tile * LANES, LANES)
            there = pl.ds(tile * LANES, LANES)
            q = q_ref[group, :, there]
            if dx_ref is not None:
                dx_ref[:, here] = (part_ref[group, :, there] + wide_ref[group, 2 * seq :, there] * q).astype(bf16)
            if want_rows:
                pull = v_ref[group, 0:seq, there].astype(f32) * y_ref[group, :, there] - drive_ref[group, :, there].astype(f32) * q
                found[2].append(jnp.sum(wide_ref[group, 0:seq, there] * pull, axis=0, keepdims=True))
    return [jnp.concatenate(row, axis=1) for row in found] if want_rows else None


def place_rows(found, block, heads, out_ref, earlier_ref):
    gains, skips, logs = found
    height = out_ref.shape[0]
    share = out_ref.shape[1] - LANES
    parts = gains.shape[1] // share
    width = gains.shape[1] // heads
    row = lax.broadcasted_iota(jnp.int32, (height, share), 0) - block * parts
    mine = jnp.zeros((height, share), f32)
    for part in range(parts):
        piece = jnp.broadcast_to(gains[:, part * share : (part + 1) * share], (height, share))
        mine = jnp.where(row == part, piece, mine)
    lane = lax.broadcasted_iota(jnp.int32, (1, LANES), 1)
    sums = jnp.zeros((1, LANES), f32)
    for tile in range(gains.shape[1] // LANES):
        here = slice(tile * LANES, (tile + 1) * LANES)
        for kind, rows in enumerate((skips, logs)):
            whole = rows[:, here]
            for side in range(LANES // width):
                inside = (lane >= side * width) & (lane < (side + 1) * width)
                total = jnp.sum(jnp.where(inside, whole, 0.0), axis=1, keepdims=True)
                head = tile * (LANES // width) + side
                sums = jnp.where(lane == (2 * kind + block) * heads + head, total, sums)
    top = lax.broadcasted_iota(jnp.int32, (height, LANES), 0) == 0
    sums = jnp.where(top, jnp.broadcast_to(sums, (height, LANES)), 0.0)
    if earlier_ref is not None:
        mine = mine + earlier_ref[:, 0:share]
        sums = sums + earlier_ref[:, share:]
    out_ref[:, 0:share] = mine
    out_ref[:, share:] = sums


def backward_first(*refs):
    backward(*refs[:7], refs[8:], refs[7], False)


def rows_first(block_ref, *refs):
    heads = refs[6].shape[1] // 3
    place_rows(backward(*refs[:7], refs[8:], None, True), block_ref[0], heads, refs[7], None)


def backward_last(
    block_ref,
    earlier_ref,
    g_ref,
    slope_ref,
    normed_ref,
    scores_ref,
    gain_ref,
    wx_ref,
    skips_ref,
    moved_ref,
    mixed_ref,
    driven_ref,
    out_ref,
    packet_ref,
    dx_ref,
    v_ref,
    q_ref,
    part_ref,
    sem,
):
    seq, chan = normed_ref.shape
    groups = scores_ref.shape[0]
    per_group = chan // groups
    tiles = per_group // LANES
    found = [[], [], []]
    moves = []
    for group in range(groups):
        total = jnp.zeros((seq, LANES), f32)
        for tile in range(tiles):
            here = pl.ds(group * per_group + tile * LANES, LANES)
            gn = g_ref[:, here].astype(f32) * normed_ref[:, here].astype(f32)
            total = total + gn * gain_ref[0:1, here]
            found[0].append(jnp.sum(gn, axis=0, keepdims=True))
        mean = jnp.sum(total, axis=1, keepdims=True) * (1.0 / per_group)
        for tile in range(tiles):
            here = pl.ds(group * per_group + tile * LANES, LANES)
            there = pl.ds(tile * LANES, LANES)
            g = g_ref[:, here].astype(f32)
            v = slope_ref[:, here] * (g * gain_ref[0:1, here] - normed_ref[:, here].astype(f32) * mean)
            v_ref[group, :, there] = v.astype(bf16)
            part_ref[group, :, there] = g + skips_ref[:, here] * v
            found[1].append(jnp.sum(moved_ref[:, here] * v, axis=0, keepdims=True))
        q_ref[group] = jnp.dot(scores_ref[group, 1], v_ref[group], preferred_element_type=f32)
    for group in range(groups):
        for tile in range(tiles):
            here = pl.ds(group * per_group + tile * LANES, LANES)
            there = pl.ds(tile * LANES, LANES)
            q = q_ref[group, :, there]
            dx_ref[:, here] = (part_ref[group, :, there] + wx_ref[:, here] * q).astype(bf16)
            pull = v_ref[group, :, there].astype(f32) * mixed_ref[:, here] - driven_ref[:, here] * q
            found[2].append(jnp.sum(pull, axis=0, keepdims=True))
        here = pl.ds(group * per_group, per_group)
        moves.append(pltpu.make_async_copy(dx_ref.at[:, here], out_ref.at[:, here], sem.at[group]))
        moves[-1].start()
    rows = [jnp.concatenate(row, axis=1) for row in found]
    place_rows(rows, block_ref[1], chan // WIDTH, packet_ref, earlier_ref)
    for move in moves:
        move.wait()


def finish(me_ref, x_ref, gathered_ref, out_ref, alog_out, dskip_out, gain_out, alog_ref, dskip_ref, gain_ref, sem):
    parts, _, share = x_ref.shape
    moves = [
        pltpu.make_async_copy(x_ref.at[i], out_ref.at[0, 0, :, pl.ds(i * share, share)], sem.at[i]) for i in range(parts)
    ]
    for move in moves:
        move.start()
    me = me_ref[0]
    total = sum(gathered_ref[i] for i in range(gathered_ref.shape[0]))
    lanes = gain_ref.shape[2]
    replicas = total.shape[0] // 2
    held = alog_ref.shape[2]
    for block in range(2):
        row = total[block * replicas : block * replicas + 1, 0:lanes]
        skip, log = [total[0:1, lanes + (kind * 2 + block) * replicas * held :] for kind in range(2)]
        skips, logs = skip[:, 0:held], log[:, 0:held]
        for other in range(1, replicas):
            at = block * replicas + other
            row = jnp.where(me == other, total[at : at + 1, 0:lanes], row)
            skips = jnp.where(me == other, skip[:, other * held : (other + 1) * held], skips)
            logs = jnp.where(me == other, log[:, other * held : (other + 1) * held], logs)
        gain_ref[0, block : block + 1] = row
        dskip_ref[0, block : block + 1] = skips
        alog_ref[0, block : block + 1] = logs
    for i, (src, dst) in enumerate(((alog_ref, alog_out), (dskip_ref, dskip_out), (gain_ref, gain_out))):
        moves.append(pltpu.make_async_copy(src, dst, sem.at[parts + i]))
        moves[-1].start()
    for move in moves:
        move.wait()


def relay_out(x_ref, out_ref, held_ref, came, gone):
    parts, _, share = out_ref.shape
    ins = [
        pltpu.make_async_copy(x_ref.at[0, 0, :, pl.ds(i * share, share)], held_ref.at[i], came.at[i]) for i in range(parts)
    ]
    outs = [pltpu.make_async_copy(held_ref.at[i], out_ref.at[i], gone.at[i]) for i in range(parts)]
    for copy in ins:
        copy.start()
    for first, second in zip(ins, outs):
        first.wait()
        second.start()
    for copy in outs:
        copy.wait()


in_vmem = pl.BlockSpec(memory_space=pltpu.VMEM)
in_smem = pl.BlockSpec(memory_space=pltpu.SMEM)
in_any = pl.BlockSpec(memory_space=pl.ANY)
MIB = 1 << 20


def sized(shape, dtype):
    return jax.ShapeDtypeStruct(tuple(shape), dtype)


def call(kernel, name, in_specs, out_specs, out_shape, scratch=(), grant=16, cost=1):
    return pl.pallas_call(
        kernel,
        in_specs=in_specs,
        out_specs=out_specs,
        out_shape=out_shape,
        scratch_shapes=list(scratch),
        compiler_params=pltpu.CompilerParams(vmem_limit_bytes=grant * MIB),
        cost_estimate=pl.CostEstimate(flops=1000, bytes_accessed=cost * 1000 * 1000, transcendentals=0),
        name=name,
    )


def run_forward(tick, block_table, entry_table, x, z, dt, b, c, alog, dskip, gain):
    seq, chan = x.shape[3:]
    groups = b.shape[4]
    heads = dt.shape[3]
    wide = (groups, seq, chan // groups)
    flat = sized((seq, chan), f32)
    outs = [flat, sized((seq, chan), bf16), sized((groups, 3, seq, seq), bf16), sized((2, chan), f32)]
    if tick:
        outs += [flat] * 5
        scratch = [pltpu.VMEM((groups, 2 * seq, chan // groups), f32), pltpu.VMEM((seq, chan), bf16)]
    else:
        outs += [sized((seq, chan), bf16), sized((seq, 3 * heads), f32)]
        scratch = []
    scratch += [
        pltpu.VMEM((seq, chan), bf16),
        pltpu.VMEM(dt.shape[3:], f32),
        pltpu.VMEM(b.shape[3:], bf16),
        pltpu.VMEM(c.shape[3:], bf16),
        pltpu.VMEM((groups, 3 * seq, chan // groups), bf16),
    ]
    scratch += [pltpu.VMEM(wide, f32)] * 5 + [pltpu.SemaphoreType.DMA((5,))]
    in_specs = [in_smem] * 2 + [in_any] * 5 + [in_vmem] * 3
    far = [pltpu.with_memory_space_constraint(a, pltpu.HBM) for a in (x, z, dt, b, c)]
    return call(partial(forward, tick), "forward", in_specs, [in_vmem] * len(outs), outs, scratch, 24, 12)(
        block_table, entry_table, *far, alog, dskip, gain
    )


def backward_scratch(seq, chan, groups):
    wide = (groups, seq, chan // groups)
    tall = (groups, 3 * seq, chan // groups)
    return [pltpu.VMEM(wide, bf16), pltpu.VMEM(tall, bf16)] + [pltpu.VMEM(wide, f32)] * 3 + [pltpu.VMEM(tall, f32)]


def shards(
    grad_in,
    saved_x,
    saved_z,
    saved_dt,
    saved_b,
    saved_c,
    a_log,
    dskip,
    gain,
    block_table,
    entry_table,
):
    parts = lax.axis_size("tensor")
    replicas = lax.axis_size("dp")
    tokens, channels = grad_in.shape[2:]
    share = channels // parts
    seq = tokens * parts
    heads = a_log.shape[2]
    blocks = a_log.shape[1]
    packet = sized((blocks * replicas, share // replicas + LANES), f32)
    block_table = block_table.reshape(-1)
    entry_table = entry_table.reshape(-1)
    steps = jnp.swapaxes(saved_dt, 3, 4)
    me = lax.axis_index("dp").reshape(1)
    staged = call(
        relay_out,
        "relay_out",
        [in_any],
        in_any,
        sized((parts, tokens, share), bf16),
        [pltpu.VMEM((parts, tokens, share), bf16)] + [pltpu.SemaphoreType.DMA((parts,))] * 2,
    )(pltpu.with_memory_space_constraint(grad_in, pltpu.HBM))
    g = lax.all_to_all(staged, "tensor", split_axis=0, concat_axis=0, tiled=True).reshape(seq, share)
    first, last = [
        run_forward(tick, block_table, entry_table, saved_x, saved_z, steps, saved_b, saved_c, a_log, dskip, gain)
        for tick in range(2)
    ]
    scratch = backward_scratch(seq, share, saved_b.shape[4])
    dx = call(backward_first, "backward_first", [in_vmem] * 7, in_vmem, sized((seq, share), bf16), scratch, 20, 6)(g, *first)
    earlier = call(rows_first, "rows_first", [in_smem] + [in_vmem] * 7, in_vmem, packet, scratch, 20, 6)(
        block_table, g, *first
    )
    g = passed_along(dx, "pipe", -1)
    dx, rows = call(
        backward_last,
        "backward_last",
        [in_smem] + [in_vmem] * 11,
        [in_any, in_vmem],
        [pltpu.HBM((seq, share), bf16), packet],
        [pltpu.VMEM((seq, share), bf16), scratch[0], *scratch[2:4], pltpu.SemaphoreType.DMA((saved_b.shape[4],))],
        20,
        6,
    )(block_table, earlier, g, *last)
    out = lax.all_to_all(dx.reshape(parts, tokens, share), "tensor", split_axis=0, concat_axis=0, tiled=True)
    rows = lax.all_gather(rows, "dp")
    shapes = [(1, blocks, heads // replicas)] * 2 + [(1, blocks, share // replicas)]
    out, grad_alog, grad_dskip, grad_gain = call(
        finish,
        "finish",
        [in_smem] + [in_vmem] * 2,
        [in_any] * 4,
        [sized(grad_in.shape, bf16)] + [sized(shape, f32) for shape in shapes],
        [pltpu.VMEM(shape, f32) for shape in shapes] + [pltpu.SemaphoreType.DMA((parts + 3,))],
    )(me, out, rows)
    return (out, grad_alog, grad_dskip, grad_gain)


def solution(mesh):
    placed = (
        P("pipe", "dp", "tensor", None),
        P("pipe", "dp", None, None, "tensor"),
        P("pipe", "dp", None, None, "tensor"),
        P("pipe", "dp", None, None, "tensor"),
        P("pipe", "dp", None, None, "tensor", None),
        P("pipe", "dp", None, None, "tensor", None),
        P("pipe", None, "tensor"),
        P("pipe", None, "tensor"),
        P("pipe", None, "tensor"),
        P(None, "pipe", "dp"),
        P(None, "pipe", "dp"),
    )
    return jax.shard_map(
        shards,
        mesh=mesh,
        in_specs=placed,
        out_specs=(
            P("pipe", "dp", "tensor", None),
            P("pipe", None, ("tensor", "dp")),
            P("pipe", None, ("tensor", "dp")),
            P("pipe", None, ("tensor", "dp")),
        ),
        check_vma=False,
    )
```

```python
from functools import partial

import jax
import jax.numpy as jnp
from jax import lax
from jax.experimental import pallas as pl
from jax.experimental.pallas import tpu as pltpu
from jax.sharding import PartitionSpec as P

eps = 1e-05
f32 = jnp.float32
bf16 = jnp.bfloat16
LANES = 128
WIDTH = 64
ORDERS = ((0, 1, 2, 3), (2, 0, 3, 1))


def passed_along(block, axis, distance):
    devices = range(lax.axis_size(axis))
    route = [((i - distance) % len(devices), i) for i in devices]
    return lax.ppermute(block, axis, route)


def thirds(value):
    high = value.astype(bf16)
    rest = value - high.astype(f32)
    middle = rest.astype(bf16)
    return high, middle, (rest - middle.astype(f32)).astype(bf16)


def place_of(member, core):
    places = [order.index(member) for order in ORDERS]
    return jnp.where(core == 0, places[0], places[1])


def of_block(ref, block, here=slice(None)):
    rows = ref[0, :, here]
    row = rows[0:1]
    for other in range(1, rows.shape[0]):
        row = jnp.where(block == other, rows[other : other + 1], row)
    return row


def spread_map(heads, width):
    first = lax.broadcasted_iota(jnp.int32, (heads, heads * width), 0) * width
    lane = lax.broadcasted_iota(jnp.int32, (heads, heads * width), 1)
    one_hot = jnp.where((lane >= first) & (lane < first + width), 1.0, 0.0).astype(bf16)
    return jnp.concatenate([one_hot] * 3, axis=0)


def spread(values, one_hot):
    return jnp.dot(jnp.concatenate(thirds(values), axis=1), one_hot, preferred_element_type=f32)


def halves(value):
    high = value.astype(bf16)
    return high, (value - high.astype(f32)).astype(bf16)


def forward(
    tick,
    block_ref,
    entry_ref,
    x_hbm,
    z_hbm,
    dt_hbm,
    b_hbm,
    c_hbm,
    alog_ref,
    dskip_ref,
    gain_ref,
    slope_ref,
    normed_ref,
    scores_ref,
    rows_ref,
    *refs,
):
    if tick:
        wx_out, skips_ref, moved_ref, mixed_ref, driven_ref, wide_ref, x_ref, *refs = refs
    else:
        x_ref, heads_ref, *refs = refs
    z_ref, dt_ref, b_ref, c_ref, drive_ref, wx_ref, ec_ref, y_ref, gated_ref, gate_ref, sem = refs
    block = block_ref[tick]
    entry = entry_ref[tick]
    moves = [
        pltpu.make_async_copy(src.at[0, 0, entry], dst, sem.at[i])
        for i, (src, dst) in enumerate(
            ((dt_hbm, dt_ref), (b_hbm, b_ref), (c_hbm, c_ref), (x_hbm, x_ref), (z_hbm, z_ref))
        )
    ]
    for move in moves:
        move.start()
    seq, chan = normed_ref.shape
    groups = scores_ref.shape[0]
    heads = dt_ref.shape[0]
    width = chan // heads
    per_group = chan // groups
    held = heads // groups
    tiles = per_group // LANES
    row = lax.broadcasted_iota(jnp.int32, (seq, seq), 0)
    col = lax.broadcasted_iota(jnp.int32, (seq, seq), 1)
    rate = jnp.exp(of_block(alog_ref, block))
    one_hot = spread_map(held, width)
    rows_ref[0:1] = of_block(gain_ref, block)
    skips = jnp.broadcast_to(of_block(dskip_ref, block), (8, heads))
    for group in range(groups):
        mine = slice(group * held, (group + 1) * held)
        rows_ref[1:2, pl.ds(group * per_group, per_group)] = spread(skips[:, mine], one_hot)[0:1]
    moves[0].wait()
    lower = (row >= col).astype(bf16)
    same = (row == col).astype(bf16)
    taken = jnp.concatenate([jnp.concatenate([lower] * 3, axis=1), jnp.concatenate([same] * 3, axis=1)], axis=0)
    steps = jnp.concatenate(thirds(dt_ref[...]), axis=1)
    steps = lax.dot_general(taken, steps, (((1,), (1,)), ((), ())), preferred_element_type=f32)
    cum = -steps[0:seq] * rate
    grow = jnp.exp(-cum)
    fall = jnp.exp(cum)
    weight = grow * steps[seq:]
    if not tick:
        heads_ref[:, 0:heads] = cum
        heads_ref[:, heads : 2 * heads] = grow
        heads_ref[:, 2 * heads : 3 * heads] = weight
    for group in range(groups):
        mine = slice(group * held, (group + 1) * held)
        both = spread(jnp.concatenate([weight[:, mine], fall[:, mine]], axis=0), one_hot)
        wx_ref[group] = both[0:seq]
        ec_ref[group] = both[seq:]
        if tick:
            wide_ref[group] = spread(jnp.concatenate([grow[:, mine], cum[:, mine]], axis=0), one_hot)
    moves[1].wait()
    moves[2].wait()
    mixers = []
    for group in range(groups):
        bmat = b_ref[:, group, :]
        cmat = c_ref[:, group, :]
        st = lax.dot_general(bmat, cmat, (((1,), (1,)), ((), ())), preferred_element_type=f32)
        scores_ref[group, 1], scores_ref[group, 2] = halves(jnp.where(row <= col, st, 0.0))
        scores = lax.dot_general(cmat, bmat, (((1,), (1,)), ((), ())), preferred_element_type=f32)
        high, low = halves(jnp.where(row >= col, scores, 0.0))
        scores_ref[group, 0] = high
        mixers.append(jnp.concatenate([high, high, low], axis=1))
    moves[3].wait()
    for group in range(groups):
        for tile in range(tiles):
            here = pl.ds(group * per_group + tile * LANES, LANES)
            there = pl.ds(tile * LANES, LANES)
            x = x_ref[:, here].astype(f32)
            wx = wx_ref[group, :, there]
            high, low = halves(wx * x)
            if tick:
                wx_out[:, here] = wx
                grown = wide_ref[group, 0:seq, there]
                skips_ref[:, here] = grown * rows_ref[1:2, here]
                moved_ref[:, here] = grown * x
                driven_ref[:, here] = wide_ref[group, seq:, there] * high.astype(f32)
            drive_ref[group, 0:seq, there] = high
            drive_ref[group, seq : 2 * seq, there] = low
            drive_ref[group, 2 * seq :, there] = high
        if tick:
            y_ref[group] = jnp.dot(scores_ref[group, 0], drive_ref[group, 0:seq], preferred_element_type=f32)
            for tile in range(tiles):
                here = pl.ds(group * per_group + tile * LANES, LANES)
                there = pl.ds(tile * LANES, LANES)
                mixed_ref[:, here] = wide_ref[group, seq:, there] * y_ref[group, :, there]
        y_ref[group] = jnp.dot(mixers[group], drive_ref[group], preferred_element_type=f32)
    moves[4].wait()
    for group in range(groups):
        total = jnp.zeros((seq, LANES), f32)
        for tile in range(tiles):
            here = pl.ds(group * per_group + tile * LANES, LANES)
            there = pl.ds(tile * LANES, LANES)
            ec = ec_ref[group, :, there]
            z = z_ref[:, here].astype(f32)
            gate = z * jax.nn.sigmoid(z)
            gated = (ec * y_ref[group, :, there] + rows_ref[1:2, here] * x_ref[:, here].astype(f32)) * gate
            total = total + gated * gated
            gated_ref[group, :, there] = gated
            gate_ref[group, :, there] = ec * gate
        scale = lax.rsqrt(jnp.sum(total, axis=1, keepdims=True) * (1.0 / per_group) + eps)
        for tile in range(tiles):
            here = pl.ds(group * per_group + tile * LANES, LANES)
            there = pl.ds(tile * LANES, LANES)
            normed_ref[:, here] = (gated_ref[group, :, there] * scale).astype(bf16)
            slope_ref[:, here] = gate_ref[group, :, there] * scale


def backward(me_ref, g_ref, slope_ref, normed_ref, scores_ref, rows_ref, x_ref, heads_ref, scratch, dx_ref, want_rows):
    drive_ref, v_ref, q_ref, y_ref, part_ref, wide_ref = scratch
    seq, chan = normed_ref.shape
    groups = scores_ref.shape[0]
    heads = heads_ref.shape[1] // 3
    per_group = chan // groups
    held = heads // groups
    width = per_group // held
    tiles = per_group // LANES
    one_hot = spread_map(held, width)
    found = [[], [], []]
    means = []
    places = [place_of(member, me_ref[0] % 2) for member in range(g_ref.shape[0])]

    def gradient(here):
        return jnp.concatenate([g_ref[place, :, here] for place in places], axis=0).astype(f32)

    for group in range(groups):
        total = jnp.zeros((seq, LANES), f32)
        for tile in range(tiles):
            here = pl.ds(group * per_group + tile * LANES, LANES)
            gn = gradient(here) * normed_ref[:, here].astype(f32)
            total = total + gn * rows_ref[0:1, here]
            if want_rows:
                found[0].append(jnp.sum(gn, axis=0, keepdims=True))
        means.append(jnp.sum(total, axis=1, keepdims=True) * (1.0 / per_group))
        kinds = range(3) if want_rows else range(1, 3)
        factors = [heads_ref[:, kind * heads + group * held : kind * heads + (group + 1) * held] for kind in kinds]
        wide_ref[group, kinds[0] * seq :] = spread(jnp.concatenate(factors, axis=0), one_hot)
    for group in range(groups):
        for tile in range(tiles):
            here = pl.ds(group * per_group + tile * LANES, LANES)
            there = pl.ds(tile * LANES, LANES)
            g = gradient(here)
            v = slope_ref[:, here] * (g * rows_ref[0:1, here] - normed_ref[:, here].astype(f32) * means[group])
            high = v.astype(bf16)
            v_ref[group, 0:seq, there] = high
            if not want_rows:
                v_ref[group, seq : 2 * seq, there] = (v - high.astype(f32)).astype(bf16)
                v_ref[group, 2 * seq :, there] = high
            dy = wide_ref[group, seq : 2 * seq, there] * v
            if dx_ref is not None:
                part_ref[group, :, there] = g + rows_ref[1:2, here] * dy
            if want_rows:
                x = x_ref[:, here].astype(f32)
                found[1].append(jnp.sum(dy * x, axis=0, keepdims=True))
                drive_ref[group, :, there] = (wide_ref[group, 2 * seq :, there] * x).astype(bf16)
        if want_rows:
            q_ref[group] = jnp.dot(scores_ref[group, 1], v_ref[group, 0:seq], preferred_element_type=f32)
            y_ref[group] = jnp.dot(scores_ref[group, 0], drive_ref[group], preferred_element_type=f32)
        else:
            high = scores_ref[group, 1]
            mixer = jnp.concatenate([high, high, scores_ref[group, 2]], axis=1)
            q_ref[group] = jnp.dot(mixer, v_ref[group], preferred_element_type=f32)
    for group in range(groups):
        for tile in range(tiles):
            here = pl.ds(group * per_group + tile * LANES, LANES)
            there = pl.ds(tile * LANES, LANES)
            q = q_ref[group, :, there]
            if dx_ref is not None:
                dx_ref[:, here] = (part_ref[group, :, there] + wide_ref[group, 2 * seq :, there] * q).astype(bf16)
            if want_rows:
                pull = v_ref[group, 0:seq, there].astype(f32) * y_ref[group, :, there] - drive_ref[group, :, there].astype(f32) * q
                found[2].append(jnp.sum(wide_ref[group, 0:seq, there] * pull, axis=0, keepdims=True))
    return [jnp.concatenate(row, axis=1) for row in found] if want_rows else None


def place_rows(found, block, heads, out_ref, earlier_ref):
    gains, skips, logs = found
    height = out_ref.shape[0]
    share = out_ref.shape[1] - LANES
    parts = gains.shape[1] // share
    width = gains.shape[1] // heads
    row = lax.broadcasted_iota(jnp.int32, (height, share), 0) - block * parts
    mine = jnp.zeros((height, share), f32)
    for part in range(parts):
        piece = jnp.broadcast_to(gains[:, part * share : (part + 1) * share], (height, share))
        mine = jnp.where(row == part, piece, mine)
    lane = lax.broadcasted_iota(jnp.int32, (1, LANES), 1)
    sums = jnp.zeros((1, LANES), f32)
    for tile in range(gains.shape[1] // LANES):
        here = slice(tile * LANES, (tile + 1) * LANES)
        for kind, rows in enumerate((skips, logs)):
            whole = rows[:, here]
            for side in range(LANES // width):
                inside = (lane >= side * width) & (lane < (side + 1) * width)
                total = jnp.sum(jnp.where(inside, whole, 0.0), axis=1, keepdims=True)
                head = tile * (LANES // width) + side
                sums = jnp.where(lane == (2 * kind + block) * heads + head, total, sums)
    top = lax.broadcasted_iota(jnp.int32, (height, LANES), 0) == 0
    sums = jnp.where(top, jnp.broadcast_to(sums, (height, LANES)), 0.0)
    if earlier_ref is not None:
        mine = mine + earlier_ref[:, 0:share]
        sums = sums + earlier_ref[:, share:]
    out_ref[:, 0:share] = mine
    out_ref[:, share:] = sums


def backward_first(*refs):
    backward(*refs[:8], refs[9:], refs[8], False)


def rows_first(block_ref, *refs):
    heads = refs[7].shape[1] // 3
    place_rows(backward(*refs[:8], refs[9:], None, True), block_ref[0], heads, refs[8], None)


def backward_last(
    block_ref,
    earlier_ref,
    g_ref,
    slope_ref,
    normed_ref,
    scores_ref,
    gain_ref,
    wx_ref,
    skips_ref,
    moved_ref,
    mixed_ref,
    driven_ref,
    out_ref,
    packet_ref,
    dx_ref,
    v_ref,
    q_ref,
    part_ref,
    sem,
):
    seq, chan = normed_ref.shape
    groups = scores_ref.shape[0]
    per_group = chan // groups
    tiles = per_group // LANES
    found = [[], [], []]
    moves = []
    for group in range(groups):
        total = jnp.zeros((seq, LANES), f32)
        for tile in range(tiles):
            here = pl.ds(group * per_group + tile * LANES, LANES)
            gn = g_ref[:, here].astype(f32) * normed_ref[:, here].astype(f32)
            total = total + gn * gain_ref[0:1, here]
            found[0].append(jnp.sum(gn, axis=0, keepdims=True))
        mean = jnp.sum(total, axis=1, keepdims=True) * (1.0 / per_group)
        for tile in range(tiles):
            here = pl.ds(group * per_group + tile * LANES, LANES)
            there = pl.ds(tile * LANES, LANES)
            g = g_ref[:, here].astype(f32)
            v = slope_ref[:, here] * (g * gain_ref[0:1, here] - normed_ref[:, here].astype(f32) * mean)
            v_ref[group, :, there] = v.astype(bf16)
            part_ref[group, :, there] = g + skips_ref[:, here] * v
            found[1].append(jnp.sum(moved_ref[:, here] * v, axis=0, keepdims=True))
        q_ref[group] = jnp.dot(scores_ref[group, 1], v_ref[group], preferred_element_type=f32)
    for group in range(groups):
        for tile in range(tiles):
            here = pl.ds(group * per_group + tile * LANES, LANES)
            there = pl.ds(tile * LANES, LANES)
            q = q_ref[group, :, there]
            dx_ref[:, here] = (part_ref[group, :, there] + wx_ref[:, here] * q).astype(bf16)
            pull = v_ref[group, :, there].astype(f32) * mixed_ref[:, here] - driven_ref[:, here] * q
            found[2].append(jnp.sum(pull, axis=0, keepdims=True))
        here = pl.ds(group * per_group, per_group)
        moves.append(pltpu.make_async_copy(dx_ref.at[:, here], out_ref.at[:, here], sem.at[group]))
        moves[-1].start()
    rows = [jnp.concatenate(row, axis=1) for row in found]
    place_rows(rows, block_ref[1], chan // WIDTH, packet_ref, earlier_ref)
    for move in moves:
        move.wait()


def finish(me_ref, x_ref, gathered_ref, out_ref, alog_out, dskip_out, gain_out, alog_ref, dskip_ref, gain_ref, sem):
    parts, _, share = x_ref.shape
    moves = [
        pltpu.make_async_copy(x_ref.at[i], out_ref.at[0, 0, :, pl.ds(i * share, share)], sem.at[i]) for i in range(parts)
    ]
    for move in moves:
        move.start()
    me = me_ref[0]
    total = sum(gathered_ref[i] for i in range(gathered_ref.shape[0]))
    lanes = gain_ref.shape[2]
    replicas = total.shape[0] // 2
    held = alog_ref.shape[2]
    for block in range(2):
        row = total[block * replicas : block * replicas + 1, 0:lanes]
        skip, log = [total[0:1, lanes + (kind * 2 + block) * replicas * held :] for kind in range(2)]
        skips, logs = skip[:, 0:held], log[:, 0:held]
        for other in range(1, replicas):
            at = block * replicas + other
            row = jnp.where(me == other, total[at : at + 1, 0:lanes], row)
            skips = jnp.where(me == other, skip[:, other * held : (other + 1) * held], skips)
            logs = jnp.where(me == other, log[:, other * held : (other + 1) * held], logs)
        gain_ref[0, block : block + 1] = row
        dskip_ref[0, block : block + 1] = skips
        alog_ref[0, block : block + 1] = logs
    for i, (src, dst) in enumerate(((alog_ref, alog_out), (dskip_ref, dskip_out), (gain_ref, gain_out))):
        moves.append(pltpu.make_async_copy(src, dst, sem.at[parts + i]))
        moves[-1].start()
    for move in moves:
        move.wait()


def relay_out(me_ref, x_ref, out_ref, held_ref, came, gone):
    parts, _, share = out_ref.shape
    ins = [
        pltpu.make_async_copy(x_ref.at[0, 0, :, pl.ds(i * share, share)], held_ref.at[i], came.at[i]) for i in range(parts)
    ]
    places = [place_of(i, me_ref[0] % 2) for i in range(parts)]
    outs = [pltpu.make_async_copy(held_ref.at[i], out_ref.at[places[i]], gone.at[i]) for i in range(parts)]
    for copy in ins:
        copy.start()
    for first, second in zip(ins, outs):
        first.wait()
        second.start()
    for copy in outs:
        copy.wait()


in_vmem = pl.BlockSpec(memory_space=pltpu.VMEM)
in_smem = pl.BlockSpec(memory_space=pltpu.SMEM)
in_any = pl.BlockSpec(memory_space=pl.ANY)
MIB = 1 << 20


def sized(shape, dtype):
    return jax.ShapeDtypeStruct(tuple(shape), dtype)


def call(kernel, name, in_specs, out_specs, out_shape, scratch=(), grant=16, cost=1):
    return pl.pallas_call(
        kernel,
        in_specs=in_specs,
        out_specs=out_specs,
        out_shape=out_shape,
        scratch_shapes=list(scratch),
        compiler_params=pltpu.CompilerParams(vmem_limit_bytes=grant * MIB),
        cost_estimate=pl.CostEstimate(flops=1000, bytes_accessed=cost * 1000 * 1000, transcendentals=0),
        name=name,
    )


def run_forward(tick, block_table, entry_table, x, z, dt, b, c, alog, dskip, gain):
    seq, chan = x.shape[3:]
    groups = b.shape[4]
    heads = dt.shape[3]
    wide = (groups, seq, chan // groups)
    flat = sized((seq, chan), f32)
    outs = [flat, sized((seq, chan), bf16), sized((groups, 3, seq, seq), bf16), sized((2, chan), f32)]
    if tick:
        outs += [flat] * 5
        scratch = [pltpu.VMEM((groups, 2 * seq, chan // groups), f32), pltpu.VMEM((seq, chan), bf16)]
    else:
        outs += [sized((seq, chan), bf16), sized((seq, 3 * heads), f32)]
        scratch = []
    scratch += [
        pltpu.VMEM((seq, chan), bf16),
        pltpu.VMEM(dt.shape[3:], f32),
        pltpu.VMEM(b.shape[3:], bf16),
        pltpu.VMEM(c.shape[3:], bf16),
        pltpu.VMEM((groups, 3 * seq, chan // groups), bf16),
    ]
    scratch += [pltpu.VMEM(wide, f32)] * 5 + [pltpu.SemaphoreType.DMA((5,))]
    in_specs = [in_smem] * 2 + [in_any] * 5 + [in_vmem] * 3
    far = [pltpu.with_memory_space_constraint(a, pltpu.HBM) for a in (x, z, dt, b, c)]
    return call(partial(forward, tick), "forward", in_specs, [in_vmem] * len(outs), outs, scratch, 24, 12)(
        block_table, entry_table, *far, alog, dskip, gain
    )


def backward_scratch(seq, chan, groups):
    wide = (groups, seq, chan // groups)
    tall = (groups, 3 * seq, chan // groups)
    return [pltpu.VMEM(wide, bf16), pltpu.VMEM(tall, bf16)] + [pltpu.VMEM(wide, f32)] * 3 + [pltpu.VMEM(tall, f32)]


def shards(
    grad_in,
    saved_x,
    saved_z,
    saved_dt,
    saved_b,
    saved_c,
    a_log,
    dskip,
    gain,
    block_table,
    entry_table,
):
    parts = lax.axis_size("tensor")
    replicas = lax.axis_size("dp")
    tokens, channels = grad_in.shape[2:]
    share = channels // parts
    seq = tokens * parts
    heads = a_log.shape[2]
    blocks = a_log.shape[1]
    packet = sized((blocks * replicas, share // replicas + LANES), f32)
    block_table = block_table.reshape(-1)
    entry_table = entry_table.reshape(-1)
    steps = jnp.swapaxes(saved_dt, 3, 4)
    me = lax.axis_index("dp").reshape(1)
    staged = call(
        relay_out,
        "relay_out",
        [in_smem, in_any],
        in_any,
        sized((parts, tokens, share), bf16),
        [pltpu.VMEM((parts, tokens, share), bf16)] + [pltpu.SemaphoreType.DMA((parts,))] * 2,
    )(me, pltpu.with_memory_space_constraint(grad_in, pltpu.HBM))
    groups = [[member * replicas + d for member in ORDERS[d % 2]] for d in range(replicas)]
    g = lax.all_to_all(staged, ("tensor", "dp"), split_axis=0, concat_axis=0, axis_index_groups=groups, tiled=True)
    first, last = [
        run_forward(tick, block_table, entry_table, saved_x, saved_z, steps, saved_b, saved_c, a_log, dskip, gain)
        for tick in range(2)
    ]
    scratch = backward_scratch(seq, share, saved_b.shape[4])
    dx = call(backward_first, "backward_first", [in_smem] + [in_vmem] * 7, in_vmem, sized((seq, share), bf16), scratch, 20, 6)(me, g, *first)
    earlier = call(rows_first, "rows_first", [in_smem] * 2 + [in_vmem] * 7, in_vmem, packet, scratch, 20, 6)(
        block_table, me, g, *first
    )
    g = passed_along(dx, "pipe", -1)
    dx, rows = call(
        backward_last,
        "backward_last",
        [in_smem] + [in_vmem] * 11,
        [in_any, in_vmem],
        [pltpu.HBM((seq, share), bf16), packet],
        [pltpu.VMEM((seq, share), bf16), scratch[0], *scratch[2:4], pltpu.SemaphoreType.DMA((saved_b.shape[4],))],
        20,
        6,
    )(block_table, earlier, g, *last)
    out = lax.all_to_all(dx.reshape(parts, tokens, share), "tensor", split_axis=0, concat_axis=0, tiled=True)
    rows = lax.all_gather(rows, "dp")
    shapes = [(1, blocks, heads // replicas)] * 2 + [(1, blocks, share // replicas)]
    out, grad_alog, grad_dskip, grad_gain = call(
        finish,
        "finish",
        [in_smem] + [in_vmem] * 2,
        [in_any] * 4,
        [sized(grad_in.shape, bf16)] + [sized(shape, f32) for shape in shapes],
        [pltpu.VMEM(shape, f32) for shape in shapes] + [pltpu.SemaphoreType.DMA((parts + 3,))],
    )(me, out, rows)
    return (out, grad_alog, grad_dskip, grad_gain)


def solution(mesh):
    placed = (
        P("pipe", "dp", "tensor", None),
        P("pipe", "dp", None, None, "tensor"),
        P("pipe", "dp", None, None, "tensor"),
        P("pipe", "dp", None, None, "tensor"),
        P("pipe", "dp", None, None, "tensor", None),
        P("pipe", "dp", None, None, "tensor", None),
        P("pipe", None, "tensor"),
        P("pipe", None, "tensor"),
        P("pipe", None, "tensor"),
        P(None, "pipe", "dp"),
        P(None, "pipe", "dp"),
    )
    return jax.shard_map(
        shards,
        mesh=mesh,
        in_specs=placed,
        out_specs=(
            P("pipe", "dp", "tensor", None),
            P("pipe", None, ("tensor", "dp")),
            P("pipe", None, ("tensor", "dp")),
            P("pipe", None, ("tensor", "dp")),
        ),
        check_vma=False,
    )
```

```python
from functools import partial

import jax
import jax.numpy as jnp
from jax import lax
from jax.experimental import pallas as pl
from jax.experimental.pallas import tpu as pltpu
from jax.sharding import PartitionSpec as P

eps = 1e-05
f32 = jnp.float32
bf16 = jnp.bfloat16
LANES = 128
WIDTH = 64
ORDERS = ((0, 1, 2, 3), (2, 0, 3, 1))


def passed_along(block, axis, distance):
    devices = range(lax.axis_size(axis))
    route = [((i - distance) % len(devices), i) for i in devices]
    return lax.ppermute(block, axis, route)


def thirds(value):
    high = value.astype(bf16)
    rest = value - high.astype(f32)
    middle = rest.astype(bf16)
    return high, middle, (rest - middle.astype(f32)).astype(bf16)


def place_of(member, core):
    places = [order.index(member) for order in ORDERS]
    return jnp.where(core == 0, places[0], places[1])


def of_block(ref, block, here=slice(None)):
    rows = ref[0, :, here]
    row = rows[0:1]
    for other in range(1, rows.shape[0]):
        row = jnp.where(block == other, rows[other : other + 1], row)
    return row


def spread_map(heads, width):
    first = lax.broadcasted_iota(jnp.int32, (heads, heads * width), 0) * width
    lane = lax.broadcasted_iota(jnp.int32, (heads, heads * width), 1)
    one_hot = jnp.where((lane >= first) & (lane < first + width), 1.0, 0.0).astype(bf16)
    return jnp.concatenate([one_hot] * 3, axis=0)


def spread(values, one_hot):
    return jnp.dot(jnp.concatenate(thirds(values), axis=1), one_hot, preferred_element_type=f32)


def halves(value):
    high = value.astype(bf16)
    return high, (value - high.astype(f32)).astype(bf16)


def forward(
    tick,
    block_ref,
    entry_ref,
    x_hbm,
    z_hbm,
    dt_hbm,
    b_hbm,
    c_hbm,
    alog_ref,
    dskip_ref,
    gain_ref,
    slope_ref,
    normed_ref,
    scores_ref,
    rows_ref,
    *refs,
):
    if tick:
        wx_out, skips_ref, moved_ref, mixed_ref, driven_ref, pushed_ref, wide_ref, x_ref, *refs = refs
    else:
        x_ref, heads_ref, *refs = refs
    z_ref, dt_ref, b_ref, c_ref, drive_ref, wx_ref, ec_ref, y_ref, gated_ref, gate_ref, sem = refs
    block = block_ref[tick]
    entry = entry_ref[tick]
    moves = [
        pltpu.make_async_copy(src.at[0, 0, entry], dst, sem.at[i])
        for i, (src, dst) in enumerate(
            ((dt_hbm, dt_ref), (b_hbm, b_ref), (c_hbm, c_ref), (x_hbm, x_ref), (z_hbm, z_ref))
        )
    ]
    for move in moves:
        move.start()
    seq, chan = normed_ref.shape
    groups = scores_ref.shape[0]
    heads = dt_ref.shape[0]
    width = chan // heads
    per_group = chan // groups
    held = heads // groups
    tiles = per_group // LANES
    row = lax.broadcasted_iota(jnp.int32, (seq, seq), 0)
    col = lax.broadcasted_iota(jnp.int32, (seq, seq), 1)
    rate = jnp.exp(of_block(alog_ref, block))
    one_hot = spread_map(held, width)
    rows_ref[0:1] = of_block(gain_ref, block)
    skips = jnp.broadcast_to(of_block(dskip_ref, block), (8, heads))
    for group in range(groups):
        mine = slice(group * held, (group + 1) * held)
        rows_ref[1:2, pl.ds(group * per_group, per_group)] = spread(skips[:, mine], one_hot)[0:1]
    moves[0].wait()
    lower = (row >= col).astype(bf16)
    same = (row == col).astype(bf16)
    taken = jnp.concatenate([jnp.concatenate([lower] * 3, axis=1), jnp.concatenate([same] * 3, axis=1)], axis=0)
    steps = jnp.concatenate(thirds(dt_ref[...]), axis=1)
    steps = lax.dot_general(taken, steps, (((1,), (1,)), ((), ())), preferred_element_type=f32)
    cum = -steps[0:seq] * rate
    grow = jnp.exp(-cum)
    fall = jnp.exp(cum)
    weight = grow * steps[seq:]
    if not tick:
        heads_ref[:, 0:heads] = cum
        heads_ref[:, heads : 2 * heads] = grow
        heads_ref[:, 2 * heads : 3 * heads] = weight
    for group in range(groups):
        mine = slice(group * held, (group + 1) * held)
        both = spread(jnp.concatenate([weight[:, mine], fall[:, mine]], axis=0), one_hot)
        wx_ref[group] = both[0:seq]
        ec_ref[group] = both[seq:]
        if tick:
            wide_ref[group] = spread(jnp.concatenate([grow[:, mine], cum[:, mine]], axis=0), one_hot)
    moves[1].wait()
    moves[2].wait()
    mixers = []
    for group in range(groups):
        bmat = b_ref[:, group, :]
        cmat = c_ref[:, group, :]
        st = lax.dot_general(bmat, cmat, (((1,), (1,)), ((), ())), preferred_element_type=f32)
        scores_ref[group, 1], scores_ref[group, 2] = halves(jnp.where(row <= col, st, 0.0))
        scores = lax.dot_general(cmat, bmat, (((1,), (1,)), ((), ())), preferred_element_type=f32)
        high, low = halves(jnp.where(row >= col, scores, 0.0))
        scores_ref[group, 0] = high
        mixers.append(jnp.concatenate([high, high, low], axis=1))
    moves[3].wait()
    for group in range(groups):
        for tile in range(tiles):
            here = pl.ds(group * per_group + tile * LANES, LANES)
            there = pl.ds(tile * LANES, LANES)
            x = x_ref[:, here].astype(f32)
            wx = wx_ref[group, :, there]
            high, low = halves(wx * x)
            if tick:
                wx_out[:, here] = wx
                grown = wide_ref[group, 0:seq, there]
                skips_ref[:, here] = grown * rows_ref[1:2, here]
                moved_ref[:, here] = grown * x
                driven_ref[:, here] = wide_ref[group, seq:, there] * high.astype(f32)
            drive_ref[group, 0:seq, there] = high
            drive_ref[group, seq : 2 * seq, there] = low
            drive_ref[group, 2 * seq :, there] = high
        if tick:
            y_ref[group] = jnp.dot(scores_ref[group, 0], drive_ref[group, 0:seq], preferred_element_type=f32)
            for tile in range(tiles):
                here = pl.ds(group * per_group + tile * LANES, LANES)
                there = pl.ds(tile * LANES, LANES)
                mixed_ref[:, here] = wide_ref[group, seq:, there] * y_ref[group, :, there]
        y_ref[group] = jnp.dot(mixers[group], drive_ref[group], preferred_element_type=f32)
    moves[4].wait()
    for group in range(groups):
        total = jnp.zeros((seq, LANES), f32)
        for tile in range(tiles):
            here = pl.ds(group * per_group + tile * LANES, LANES)
            there = pl.ds(tile * LANES, LANES)
            ec = ec_ref[group, :, there]
            z = z_ref[:, here].astype(f32)
            gate = z * jax.nn.sigmoid(z)
            gated = (ec * y_ref[group, :, there] + rows_ref[1:2, here] * x_ref[:, here].astype(f32)) * gate
            total = total + gated * gated
            gated_ref[group, :, there] = gated
            gate_ref[group, :, there] = ec * gate
        scale = lax.rsqrt(jnp.sum(total, axis=1, keepdims=True) * (1.0 / per_group) + eps)
        for tile in range(tiles):
            here = pl.ds(group * per_group + tile * LANES, LANES)
            there = pl.ds(tile * LANES, LANES)
            normed = (gated_ref[group, :, there] * scale).astype(bf16)
            slope = gate_ref[group, :, there] * scale
            normed_ref[:, here] = normed
            if tick:
                slope_ref[:, here] = slope * rows_ref[0:1, here]
                pushed_ref[:, here] = slope * normed.astype(f32)
            else:
                slope_ref[:, here] = slope


def backward(me_ref, g_ref, slope_ref, normed_ref, scores_ref, rows_ref, x_ref, heads_ref, scratch, dx_ref, want_rows):
    drive_ref, v_ref, q_ref, y_ref, part_ref, wide_ref = scratch
    seq, chan = normed_ref.shape
    groups = scores_ref.shape[0]
    heads = heads_ref.shape[1] // 3
    per_group = chan // groups
    held = heads // groups
    width = per_group // held
    tiles = per_group // LANES
    one_hot = spread_map(held, width)
    found = [[], [], []]
    means = []
    places = [place_of(member, me_ref[0] % 2) for member in range(g_ref.shape[0])]

    def gradient(here):
        return jnp.concatenate([g_ref[place, :, here] for place in places], axis=0).astype(f32)

    for group in range(groups):
        total = jnp.zeros((seq, LANES), f32)
        for tile in range(tiles):
            here = pl.ds(group * per_group + tile * LANES, LANES)
            gn = gradient(here) * normed_ref[:, here].astype(f32)
            total = total + gn * rows_ref[0:1, here]
            if want_rows:
                found[0].append(jnp.sum(gn, axis=0, keepdims=True))
        means.append(jnp.sum(total, axis=1, keepdims=True) * (1.0 / per_group))
        kinds = range(3) if want_rows else range(1, 3)
        factors = [heads_ref[:, kind * heads + group * held : kind * heads + (group + 1) * held] for kind in kinds]
        wide_ref[group, kinds[0] * seq :] = spread(jnp.concatenate(factors, axis=0), one_hot)
    for group in range(groups):
        for tile in range(tiles):
            here = pl.ds(group * per_group + tile * LANES, LANES)
            there = pl.ds(tile * LANES, LANES)
            g = gradient(here)
            v = slope_ref[:, here] * (g * rows_ref[0:1, here] - normed_ref[:, here].astype(f32) * means[group])
            high = v.astype(bf16)
            v_ref[group, 0:seq, there] = high
            if not want_rows:
                v_ref[group, seq : 2 * seq, there] = (v - high.astype(f32)).astype(bf16)
                v_ref[group, 2 * seq :, there] = high
            dy = wide_ref[group, seq : 2 * seq, there] * v
            if dx_ref is not None:
                part_ref[group, :, there] = g + rows_ref[1:2, here] * dy
            if want_rows:
                x = x_ref[:, here].astype(f32)
                found[1].append(jnp.sum(dy * x, axis=0, keepdims=True))
                drive_ref[group, :, there] = (wide_ref[group, 2 * seq :, there] * x).astype(bf16)
        if want_rows:
            q_ref[group] = jnp.dot(scores_ref[group, 1], v_ref[group, 0:seq], preferred_element_type=f32)
            y_ref[group] = jnp.dot(scores_ref[group, 0], drive_ref[group], preferred_element_type=f32)
        else:
            high = scores_ref[group, 1]
            mixer = jnp.concatenate([high, high, scores_ref[group, 2]], axis=1)
            q_ref[group] = jnp.dot(mixer, v_ref[group], preferred_element_type=f32)
    for group in range(groups):
        for tile in range(tiles):
            here = pl.ds(group * per_group + tile * LANES, LANES)
            there = pl.ds(tile * LANES, LANES)
            q = q_ref[group, :, there]
            if dx_ref is not None:
                dx_ref[:, here] = (part_ref[group, :, there] + wide_ref[group, 2 * seq :, there] * q).astype(bf16)
            if want_rows:
                pull = v_ref[group, 0:seq, there].astype(f32) * y_ref[group, :, there] - drive_ref[group, :, there].astype(f32) * q
                found[2].append(jnp.sum(wide_ref[group, 0:seq, there] * pull, axis=0, keepdims=True))
    return [jnp.concatenate(row, axis=1) for row in found] if want_rows else None


def place_rows(found, block, heads, out_ref, earlier_ref):
    gains, skips, logs = found
    height = out_ref.shape[0]
    share = out_ref.shape[1] - LANES
    parts = gains.shape[1] // share
    width = gains.shape[1] // heads
    row = lax.broadcasted_iota(jnp.int32, (height, share), 0) - block * parts
    mine = jnp.zeros((height, share), f32)
    for part in range(parts):
        piece = jnp.broadcast_to(gains[:, part * share : (part + 1) * share], (height, share))
        mine = jnp.where(row == part, piece, mine)
    lane = lax.broadcasted_iota(jnp.int32, (1, LANES), 1)
    sums = jnp.zeros((1, LANES), f32)
    for tile in range(gains.shape[1] // LANES):
        here = slice(tile * LANES, (tile + 1) * LANES)
        for kind, rows in enumerate((skips, logs)):
            whole = rows[:, here]
            for side in range(LANES // width):
                inside = (lane >= side * width) & (lane < (side + 1) * width)
                total = jnp.sum(jnp.where(inside, whole, 0.0), axis=1, keepdims=True)
                head = tile * (LANES // width) + side
                sums = jnp.where(lane == (2 * kind + block) * heads + head, total, sums)
    top = lax.broadcasted_iota(jnp.int32, (height, LANES), 0) == 0
    sums = jnp.where(top, jnp.broadcast_to(sums, (height, LANES)), 0.0)
    if earlier_ref is not None:
        mine = mine + earlier_ref[:, 0:share]
        sums = sums + earlier_ref[:, share:]
    out_ref[:, 0:share] = mine
    out_ref[:, share:] = sums


def backward_first(*refs):
    backward(*refs[:8], refs[9:], refs[8], False)


def rows_first(block_ref, *refs):
    heads = refs[7].shape[1] // 3
    place_rows(backward(*refs[:8], refs[9:], None, True), block_ref[0], heads, refs[8], None)


def backward_last(
    block_ref,
    earlier_ref,
    g_ref,
    slope_ref,
    normed_ref,
    scores_ref,
    gain_ref,
    wx_ref,
    skips_ref,
    moved_ref,
    mixed_ref,
    driven_ref,
    pushed_ref,
    out_ref,
    packet_ref,
    dx_ref,
    v_ref,
    q_ref,
    part_ref,
    sem,
):
    seq, chan = normed_ref.shape
    groups = scores_ref.shape[0]
    per_group = chan // groups
    tiles = per_group // LANES
    found = [[], [], []]
    moves = []
    for group in range(groups):
        total = jnp.zeros((seq, LANES), f32)
        for tile in range(tiles):
            here = pl.ds(group * per_group + tile * LANES, LANES)
            gn = g_ref[:, here].astype(f32) * normed_ref[:, here].astype(f32)
            total = total + gn * gain_ref[0:1, here]
            found[0].append(jnp.sum(gn, axis=0, keepdims=True))
        mean = jnp.sum(total, axis=1, keepdims=True) * (1.0 / per_group)
        for tile in range(tiles):
            here = pl.ds(group * per_group + tile * LANES, LANES)
            there = pl.ds(tile * LANES, LANES)
            g = g_ref[:, here].astype(f32)
            v = slope_ref[:, here] * g - pushed_ref[:, here] * mean
            v_ref[group, :, there] = v.astype(bf16)
            part_ref[group, :, there] = g + skips_ref[:, here] * v
            found[1].append(jnp.sum(moved_ref[:, here] * v, axis=0, keepdims=True))
        q_ref[group] = jnp.dot(scores_ref[group, 1], v_ref[group], preferred_element_type=f32)
    for group in range(groups):
        for tile in range(tiles):
            here = pl.ds(group * per_group + tile * LANES, LANES)
            there = pl.ds(tile * LANES, LANES)
            q = q_ref[group, :, there]
            dx_ref[:, here] = (part_ref[group, :, there] + wx_ref[:, here] * q).astype(bf16)
            pull = v_ref[group, :, there].astype(f32) * mixed_ref[:, here] - driven_ref[:, here] * q
            found[2].append(jnp.sum(pull, axis=0, keepdims=True))
        here = pl.ds(group * per_group, per_group)
        moves.append(pltpu.make_async_copy(dx_ref.at[:, here], out_ref.at[:, here], sem.at[group]))
        moves[-1].start()
    rows = [jnp.concatenate(row, axis=1) for row in found]
    place_rows(rows, block_ref[1], chan // WIDTH, packet_ref, earlier_ref)
    for move in moves:
        move.wait()


def finish(me_ref, x_ref, gathered_ref, out_ref, alog_out, dskip_out, gain_out, alog_ref, dskip_ref, gain_ref, sem):
    parts, _, share = x_ref.shape
    moves = [
        pltpu.make_async_copy(x_ref.at[i], out_ref.at[0, 0, :, pl.ds(i * share, share)], sem.at[i]) for i in range(parts)
    ]
    for move in moves:
        move.start()
    me = me_ref[0]
    total = sum(gathered_ref[i] for i in range(gathered_ref.shape[0]))
    lanes = gain_ref.shape[2]
    replicas = total.shape[0] // 2
    held = alog_ref.shape[2]
    for block in range(2):
        row = total[block * replicas : block * replicas + 1, 0:lanes]
        skip, log = [total[0:1, lanes + (kind * 2 + block) * replicas * held :] for kind in range(2)]
        skips, logs = skip[:, 0:held], log[:, 0:held]
        for other in range(1, replicas):
            at = block * replicas + other
            row = jnp.where(me == other, total[at : at + 1, 0:lanes], row)
            skips = jnp.where(me == other, skip[:, other * held : (other + 1) * held], skips)
            logs = jnp.where(me == other, log[:, other * held : (other + 1) * held], logs)
        gain_ref[0, block : block + 1] = row
        dskip_ref[0, block : block + 1] = skips
        alog_ref[0, block : block + 1] = logs
    for i, (src, dst) in enumerate(((alog_ref, alog_out), (dskip_ref, dskip_out), (gain_ref, gain_out))):
        moves.append(pltpu.make_async_copy(src, dst, sem.at[parts + i]))
        moves[-1].start()
    for move in moves:
        move.wait()


def relay_out(me_ref, x_ref, out_ref, held_ref, came, gone):
    parts, _, share = out_ref.shape
    ins = [
        pltpu.make_async_copy(x_ref.at[0, 0, :, pl.ds(i * share, share)], held_ref.at[i], came.at[i]) for i in range(parts)
    ]
    places = [place_of(i, me_ref[0] % 2) for i in range(parts)]
    outs = [pltpu.make_async_copy(held_ref.at[i], out_ref.at[places[i]], gone.at[i]) for i in range(parts)]
    for copy in ins:
        copy.start()
    for first, second in zip(ins, outs):
        first.wait()
        second.start()
    for copy in outs:
        copy.wait()


in_vmem = pl.BlockSpec(memory_space=pltpu.VMEM)
in_smem = pl.BlockSpec(memory_space=pltpu.SMEM)
in_any = pl.BlockSpec(memory_space=pl.ANY)
MIB = 1 << 20


def sized(shape, dtype):
    return jax.ShapeDtypeStruct(tuple(shape), dtype)


def call(kernel, name, in_specs, out_specs, out_shape, scratch=(), grant=16, cost=1):
    return pl.pallas_call(
        kernel,
        in_specs=in_specs,
        out_specs=out_specs,
        out_shape=out_shape,
        scratch_shapes=list(scratch),
        compiler_params=pltpu.CompilerParams(vmem_limit_bytes=grant * MIB),
        cost_estimate=pl.CostEstimate(flops=1000, bytes_accessed=cost * 1000 * 1000, transcendentals=0),
        name=name,
    )


def run_forward(tick, block_table, entry_table, x, z, dt, b, c, alog, dskip, gain):
    seq, chan = x.shape[3:]
    groups = b.shape[4]
    heads = dt.shape[3]
    wide = (groups, seq, chan // groups)
    flat = sized((seq, chan), f32)
    outs = [flat, sized((seq, chan), bf16), sized((groups, 3, seq, seq), bf16), sized((2, chan), f32)]
    if tick:
        outs += [flat] * 6
        scratch = [pltpu.VMEM((groups, 2 * seq, chan // groups), f32), pltpu.VMEM((seq, chan), bf16)]
    else:
        outs += [sized((seq, chan), bf16), sized((seq, 3 * heads), f32)]
        scratch = []
    scratch += [
        pltpu.VMEM((seq, chan), bf16),
        pltpu.VMEM(dt.shape[3:], f32),
        pltpu.VMEM(b.shape[3:], bf16),
        pltpu.VMEM(c.shape[3:], bf16),
        pltpu.VMEM((groups, 3 * seq, chan // groups), bf16),
    ]
    scratch += [pltpu.VMEM(wide, f32)] * 5 + [pltpu.SemaphoreType.DMA((5,))]
    in_specs = [in_smem] * 2 + [in_any] * 5 + [in_vmem] * 3
    far = [pltpu.with_memory_space_constraint(a, pltpu.HBM) for a in (x, z, dt, b, c)]
    return call(partial(forward, tick), "forward", in_specs, [in_vmem] * len(outs), outs, scratch, 24, 12)(
        block_table, entry_table, *far, alog, dskip, gain
    )


def backward_scratch(seq, chan, groups):
    wide = (groups, seq, chan // groups)
    tall = (groups, 3 * seq, chan // groups)
    return [pltpu.VMEM(wide, bf16), pltpu.VMEM(tall, bf16)] + [pltpu.VMEM(wide, f32)] * 3 + [pltpu.VMEM(tall, f32)]


def shards(
    grad_in,
    saved_x,
    saved_z,
    saved_dt,
    saved_b,
    saved_c,
    a_log,
    dskip,
    gain,
    block_table,
    entry_table,
):
    parts = lax.axis_size("tensor")
    replicas = lax.axis_size("dp")
    tokens, channels = grad_in.shape[2:]
    share = channels // parts
    seq = tokens * parts
    heads = a_log.shape[2]
    blocks = a_log.shape[1]
    packet = sized((blocks * replicas, share // replicas + LANES), f32)
    block_table = block_table.reshape(-1)
    entry_table = entry_table.reshape(-1)
    steps = jnp.swapaxes(saved_dt, 3, 4)
    me = lax.axis_index("dp").reshape(1)
    staged = call(
        relay_out,
        "relay_out",
        [in_smem, in_any],
        in_any,
        sized((parts, tokens, share), bf16),
        [pltpu.VMEM((parts, tokens, share), bf16)] + [pltpu.SemaphoreType.DMA((parts,))] * 2,
    )(me, pltpu.with_memory_space_constraint(grad_in, pltpu.HBM))
    groups = [[member * replicas + d for member in ORDERS[d % 2]] for d in range(replicas)]
    g = lax.all_to_all(staged, ("tensor", "dp"), split_axis=0, concat_axis=0, axis_index_groups=groups, tiled=True)
    first, last = [
        run_forward(tick, block_table, entry_table, saved_x, saved_z, steps, saved_b, saved_c, a_log, dskip, gain)
        for tick in range(2)
    ]
    scratch = backward_scratch(seq, share, saved_b.shape[4])
    dx = call(backward_first, "backward_first", [in_smem] + [in_vmem] * 7, in_vmem, sized((seq, share), bf16), scratch, 20, 6)(me, g, *first)
    earlier = call(rows_first, "rows_first", [in_smem] * 2 + [in_vmem] * 7, in_vmem, packet, scratch, 20, 6)(
        block_table, me, g, *first
    )
    g = passed_along(dx, "pipe", -1)
    dx, rows = call(
        backward_last,
        "backward_last",
        [in_smem] + [in_vmem] * 12,
        [in_any, in_vmem],
        [pltpu.HBM((seq, share), bf16), packet],
        [pltpu.VMEM((seq, share), bf16), scratch[0], *scratch[2:4], pltpu.SemaphoreType.DMA((saved_b.shape[4],))],
        20,
        6,
    )(block_table, earlier, g, *last)
    out = lax.all_to_all(dx.reshape(parts, tokens, share), "tensor", split_axis=0, concat_axis=0, tiled=True)
    rows = lax.all_gather(rows, "dp")
    shapes = [(1, blocks, heads // replicas)] * 2 + [(1, blocks, share // replicas)]
    out, grad_alog, grad_dskip, grad_gain = call(
        finish,
        "finish",
        [in_smem] + [in_vmem] * 2,
        [in_any] * 4,
        [sized(grad_in.shape, bf16)] + [sized(shape, f32) for shape in shapes],
        [pltpu.VMEM(shape, f32) for shape in shapes] + [pltpu.SemaphoreType.DMA((parts + 3,))],
    )(me, out, rows)
    return (out, grad_alog, grad_dskip, grad_gain)


def solution(mesh):
    placed = (
        P("pipe", "dp", "tensor", None),
        P("pipe", "dp", None, None, "tensor"),
        P("pipe", "dp", None, None, "tensor"),
        P("pipe", "dp", None, None, "tensor"),
        P("pipe", "dp", None, None, "tensor", None),
        P("pipe", "dp", None, None, "tensor", None),
        P("pipe", None, "tensor"),
        P("pipe", None, "tensor"),
        P("pipe", None, "tensor"),
        P(None, "pipe", "dp"),
        P(None, "pipe", "dp"),
    )
    return jax.shard_map(
        shards,
        mesh=mesh,
        in_specs=placed,
        out_specs=(
            P("pipe", "dp", "tensor", None),
            P("pipe", None, ("tensor", "dp")),
            P("pipe", None, ("tensor", "dp")),
            P("pipe", None, ("tensor", "dp")),
        ),
        check_vma=False,
    )
```

```python
from functools import partial

import jax
import jax.numpy as jnp
from jax import lax
from jax.experimental import pallas as pl
from jax.experimental.pallas import tpu as pltpu
from jax.sharding import PartitionSpec as P

eps = 1e-05
f32 = jnp.float32
bf16 = jnp.bfloat16
LANES = 128
WIDTH = 64
ORDERS = ((0, 1, 2, 3), (2, 0, 3, 1))


def passed_along(block, axis, distance):
    devices = range(lax.axis_size(axis))
    route = [((i - distance) % len(devices), i) for i in devices]
    return lax.ppermute(block, axis, route)


def thirds(value):
    high = value.astype(bf16)
    rest = value - high.astype(f32)
    middle = rest.astype(bf16)
    return high, middle, (rest - middle.astype(f32)).astype(bf16)


def place_of(member, core):
    places = [order.index(member) for order in ORDERS]
    return jnp.where(core == 0, places[0], places[1])


def of_block(ref, block, here=slice(None)):
    rows = ref[0, :, here]
    row = rows[0:1]
    for other in range(1, rows.shape[0]):
        row = jnp.where(block == other, rows[other : other + 1], row)
    return row


def spread_map(heads, width):
    first = lax.broadcasted_iota(jnp.int32, (heads, heads * width), 0) * width
    lane = lax.broadcasted_iota(jnp.int32, (heads, heads * width), 1)
    one_hot = jnp.where((lane >= first) & (lane < first + width), 1.0, 0.0).astype(bf16)
    return jnp.concatenate([one_hot] * 3, axis=0)


def spread(values, one_hot):
    return jnp.dot(jnp.concatenate(thirds(values), axis=1), one_hot, preferred_element_type=f32)


def halves(value):
    high = value.astype(bf16)
    return high, (value - high.astype(f32)).astype(bf16)


def forward(
    tick,
    block_ref,
    entry_ref,
    x_hbm,
    z_hbm,
    dt_hbm,
    b_hbm,
    c_hbm,
    alog_ref,
    dskip_ref,
    gain_ref,
    slope_ref,
    normed_ref,
    scores_ref,
    rows_ref,
    *refs,
):
    if tick:
        wx_out, skips_ref, moved_ref, mixed_ref, driven_ref, pushed_ref, wide_ref, x_ref, *refs = refs
    else:
        x_ref, heads_ref, *refs = refs
    z_ref, dt_ref, b_ref, c_ref, drive_ref, wx_ref, ec_ref, y_ref, gated_ref, gate_ref, sem = refs
    block = block_ref[tick]
    entry = entry_ref[tick]
    moves = [
        pltpu.make_async_copy(src.at[0, 0, entry], dst, sem.at[i])
        for i, (src, dst) in enumerate(
            ((dt_hbm, dt_ref), (b_hbm, b_ref), (c_hbm, c_ref), (x_hbm, x_ref), (z_hbm, z_ref))
        )
    ]
    for move in moves:
        move.start()
    seq, chan = normed_ref.shape
    groups = scores_ref.shape[0]
    heads = dt_ref.shape[0]
    width = chan // heads
    per_group = chan // groups
    held = heads // groups
    tiles = per_group // LANES
    row = lax.broadcasted_iota(jnp.int32, (seq, seq), 0)
    col = lax.broadcasted_iota(jnp.int32, (seq, seq), 1)
    rate = jnp.exp(of_block(alog_ref, block))
    one_hot = spread_map(held, width)
    rows_ref[0:1] = of_block(gain_ref, block)
    skips = jnp.broadcast_to(of_block(dskip_ref, block), (8, heads))
    for group in range(groups):
        mine = slice(group * held, (group + 1) * held)
        rows_ref[1:2, pl.ds(group * per_group, per_group)] = spread(skips[:, mine], one_hot)[0:1]
    moves[0].wait()
    lower = (row >= col).astype(bf16)
    same = (row == col).astype(bf16)
    taken = jnp.concatenate([jnp.concatenate([lower] * 3, axis=1), jnp.concatenate([same] * 3, axis=1)], axis=0)
    steps = jnp.concatenate(thirds(dt_ref[...]), axis=1)
    steps = lax.dot_general(taken, steps, (((1,), (1,)), ((), ())), preferred_element_type=f32)
    cum = -steps[0:seq] * rate
    grow = jnp.exp(-cum)
    fall = jnp.exp(cum)
    weight = grow * steps[seq:]
    if not tick:
        heads_ref[:, 0:heads] = cum
        heads_ref[:, heads : 2 * heads] = grow
        heads_ref[:, 2 * heads : 3 * heads] = weight
    for group in range(groups):
        mine = slice(group * held, (group + 1) * held)
        both = spread(jnp.concatenate([weight[:, mine], fall[:, mine]], axis=0), one_hot)
        wx_ref[group] = both[0:seq]
        ec_ref[group] = both[seq:]
        if tick:
            wide_ref[group] = spread(jnp.concatenate([grow[:, mine], cum[:, mine]], axis=0), one_hot)
    moves[1].wait()
    moves[2].wait()
    mixers = []
    for group in range(groups):
        bmat = b_ref[:, group, :]
        cmat = c_ref[:, group, :]
        st = lax.dot_general(bmat, cmat, (((1,), (1,)), ((), ())), preferred_element_type=f32)
        scores_ref[group, 1], scores_ref[group, 2] = halves(jnp.where(row <= col, st, 0.0))
        scores = lax.dot_general(cmat, bmat, (((1,), (1,)), ((), ())), preferred_element_type=f32)
        high, low = halves(jnp.where(row >= col, scores, 0.0))
        scores_ref[group, 0] = high
        mixers.append(jnp.concatenate([high, high, low], axis=1))
    moves[3].wait()
    for group in range(groups):
        for tile in range(tiles):
            here = pl.ds(group * per_group + tile * LANES, LANES)
            there = pl.ds(tile * LANES, LANES)
            x = x_ref[:, here].astype(f32)
            wx = wx_ref[group, :, there]
            high, low = halves(wx * x)
            if tick:
                wx_out[:, here] = wx
                grown = wide_ref[group, 0:seq, there]
                skips_ref[:, here] = grown * rows_ref[1:2, here]
                moved_ref[:, here] = grown * x
                driven_ref[:, here] = wide_ref[group, seq:, there] * high.astype(f32)
            drive_ref[group, 0:seq, there] = high
            drive_ref[group, seq : 2 * seq, there] = low
            drive_ref[group, 2 * seq :, there] = high
        if tick:
            y_ref[group] = jnp.dot(scores_ref[group, 0], drive_ref[group, 0:seq], preferred_element_type=f32)
            for tile in range(tiles):
                here = pl.ds(group * per_group + tile * LANES, LANES)
                there = pl.ds(tile * LANES, LANES)
                mixed_ref[:, here] = wide_ref[group, seq:, there] * y_ref[group, :, there]
        y_ref[group] = jnp.dot(mixers[group], drive_ref[group], preferred_element_type=f32)
    moves[4].wait()
    for group in range(groups):
        total = jnp.zeros((seq, LANES), f32)
        for tile in range(tiles):
            here = pl.ds(group * per_group + tile * LANES, LANES)
            there = pl.ds(tile * LANES, LANES)
            ec = ec_ref[group, :, there]
            z = z_ref[:, here].astype(f32)
            gate = z * jax.nn.sigmoid(z)
            gated = (ec * y_ref[group, :, there] + rows_ref[1:2, here] * x_ref[:, here].astype(f32)) * gate
            total = total + gated * gated
            gated_ref[group, :, there] = gated
            gate_ref[group, :, there] = ec * gate
        scale = lax.rsqrt(jnp.sum(total, axis=1, keepdims=True) * (1.0 / per_group) + eps)
        for tile in range(tiles):
            here = pl.ds(group * per_group + tile * LANES, LANES)
            there = pl.ds(tile * LANES, LANES)
            normed = (gated_ref[group, :, there] * scale).astype(bf16)
            slope = gate_ref[group, :, there] * scale
            normed_ref[:, here] = normed
            if tick:
                slope_ref[:, here] = slope * rows_ref[0:1, here]
                pushed_ref[:, here] = slope * normed.astype(f32)
            else:
                slope_ref[:, here] = slope


def backward(me_ref, g_ref, slope_ref, normed_ref, scores_ref, rows_ref, x_ref, heads_ref, scratch, dx_ref, want_rows):
    drive_ref, v_ref, q_ref, y_ref, part_ref, wide_ref = scratch
    seq, chan = normed_ref.shape
    groups = scores_ref.shape[0]
    heads = heads_ref.shape[1] // 3
    per_group = chan // groups
    held = heads // groups
    width = per_group // held
    tiles = per_group // LANES
    one_hot = spread_map(held, width)
    found = [[], [], []]
    means = []
    places = [place_of(member, me_ref[0] % 2) for member in range(g_ref.shape[0])]

    def gradient(here):
        return jnp.concatenate([g_ref[place, :, here] for place in places], axis=0).astype(f32)

    for group in range(groups):
        total = jnp.zeros((seq, LANES), f32)
        for tile in range(tiles):
            here = pl.ds(group * per_group + tile * LANES, LANES)
            gn = gradient(here) * normed_ref[:, here].astype(f32)
            total = total + gn * rows_ref[0:1, here]
            if want_rows:
                found[0].append(jnp.sum(gn, axis=0, keepdims=True))
        means.append(jnp.sum(total, axis=1, keepdims=True) * (1.0 / per_group))
        kinds = range(3) if want_rows else range(1, 3)
        factors = [heads_ref[:, kind * heads + group * held : kind * heads + (group + 1) * held] for kind in kinds]
        wide_ref[group, kinds[0] * seq :] = spread(jnp.concatenate(factors, axis=0), one_hot)
    for group in range(groups):
        for tile in range(tiles):
            here = pl.ds(group * per_group + tile * LANES, LANES)
            there = pl.ds(tile * LANES, LANES)
            g = gradient(here)
            v = slope_ref[:, here] * (g * rows_ref[0:1, here] - normed_ref[:, here].astype(f32) * means[group])
            high = v.astype(bf16)
            v_ref[group, 0:seq, there] = high
            if not want_rows:
                v_ref[group, seq : 2 * seq, there] = (v - high.astype(f32)).astype(bf16)
                v_ref[group, 2 * seq :, there] = high
            dy = wide_ref[group, seq : 2 * seq, there] * v
            if dx_ref is not None:
                part_ref[group, :, there] = g + rows_ref[1:2, here] * dy
            if want_rows:
                x = x_ref[:, here].astype(f32)
                found[1].append(jnp.sum(dy * x, axis=0, keepdims=True))
                drive_ref[group, :, there] = (wide_ref[group, 2 * seq :, there] * x).astype(bf16)
        if want_rows:
            q_ref[group] = jnp.dot(scores_ref[group, 1], v_ref[group, 0:seq], preferred_element_type=f32)
            y_ref[group] = jnp.dot(scores_ref[group, 0], drive_ref[group], preferred_element_type=f32)
        else:
            high = scores_ref[group, 1]
            mixer = jnp.concatenate([high, high, scores_ref[group, 2]], axis=1)
            q_ref[group] = jnp.dot(mixer, v_ref[group], preferred_element_type=f32)
    for group in range(groups):
        for tile in range(tiles):
            here = pl.ds(group * per_group + tile * LANES, LANES)
            there = pl.ds(tile * LANES, LANES)
            q = q_ref[group, :, there]
            if dx_ref is not None:
                dx_ref[:, here] = (part_ref[group, :, there] + wide_ref[group, 2 * seq :, there] * q).astype(bf16)
            if want_rows:
                pull = v_ref[group, 0:seq, there].astype(f32) * y_ref[group, :, there] - drive_ref[group, :, there].astype(f32) * q
                found[2].append(jnp.sum(wide_ref[group, 0:seq, there] * pull, axis=0, keepdims=True))
    return [jnp.concatenate(row, axis=1) for row in found] if want_rows else None


def place_rows(found, block, heads, out_ref, earlier_ref):
    gains, skips, logs = found
    height = out_ref.shape[0]
    share = out_ref.shape[1] - LANES
    parts = gains.shape[1] // share
    width = gains.shape[1] // heads
    row = lax.broadcasted_iota(jnp.int32, (height, share), 0) - block * parts
    mine = jnp.zeros((height, share), f32)
    for part in range(parts):
        piece = jnp.broadcast_to(gains[:, part * share : (part + 1) * share], (height, share))
        mine = jnp.where(row == part, piece, mine)
    lane = lax.broadcasted_iota(jnp.int32, (1, LANES), 1)
    sums = jnp.zeros((1, LANES), f32)
    for tile in range(gains.shape[1] // LANES):
        here = slice(tile * LANES, (tile + 1) * LANES)
        for kind, rows in enumerate((skips, logs)):
            whole = rows[:, here]
            for side in range(LANES // width):
                inside = (lane >= side * width) & (lane < (side + 1) * width)
                total = jnp.sum(jnp.where(inside, whole, 0.0), axis=1, keepdims=True)
                head = tile * (LANES // width) + side
                sums = jnp.where(lane == (2 * kind + block) * heads + head, total, sums)
    top = lax.broadcasted_iota(jnp.int32, (height, LANES), 0) == 0
    sums = jnp.where(top, jnp.broadcast_to(sums, (height, LANES)), 0.0)
    if earlier_ref is not None:
        mine = mine + earlier_ref[:, 0:share]
        sums = sums + earlier_ref[:, share:]
    out_ref[:, 0:share] = mine
    out_ref[:, share:] = sums


def backward_first(*refs):
    backward(*refs[:8], refs[9:], refs[8], False)


def rows_first(block_ref, *refs):
    heads = refs[7].shape[1] // 3
    place_rows(backward(*refs[:8], refs[9:], None, True), block_ref[0], heads, refs[8], None)


def backward_last(
    block_ref,
    earlier_ref,
    g_ref,
    slope_ref,
    normed_ref,
    scores_ref,
    gain_ref,
    wx_ref,
    skips_ref,
    moved_ref,
    mixed_ref,
    driven_ref,
    pushed_ref,
    out_ref,
    packet_ref,
    dx_ref,
    v_ref,
    q_ref,
    part_ref,
    sem,
):
    seq, chan = normed_ref.shape
    groups = scores_ref.shape[0]
    per_group = chan // groups
    tiles = per_group // LANES
    found = [[], [], []]
    moves = []
    for group in range(groups):
        total = jnp.zeros((seq, LANES), f32)
        for tile in range(tiles):
            here = pl.ds(group * per_group + tile * LANES, LANES)
            gn = g_ref[:, here].astype(f32) * normed_ref[:, here].astype(f32)
            total = total + gn * gain_ref[0:1, here]
            found[0].append(jnp.sum(gn, axis=0, keepdims=True))
        mean = jnp.sum(total, axis=1, keepdims=True) * (1.0 / per_group)
        for tile in range(tiles):
            here = pl.ds(group * per_group + tile * LANES, LANES)
            there = pl.ds(tile * LANES, LANES)
            g = g_ref[:, here].astype(f32)
            v = slope_ref[:, here] * g - pushed_ref[:, here] * mean
            v_ref[group, :, there] = v.astype(bf16)
            part_ref[group, :, there] = g + skips_ref[:, here] * v
            found[1].append(jnp.sum(moved_ref[:, here] * v, axis=0, keepdims=True))
        q_ref[group] = jnp.dot(scores_ref[group, 1], v_ref[group], preferred_element_type=f32)
        for tile in range(tiles):
            here = pl.ds(group * per_group + tile * LANES, LANES)
            there = pl.ds(tile * LANES, LANES)
            q = q_ref[group, :, there]
            dx_ref[:, here] = (part_ref[group, :, there] + wx_ref[:, here] * q).astype(bf16)
            pull = v_ref[group, :, there].astype(f32) * mixed_ref[:, here] - driven_ref[:, here] * q
            found[2].append(jnp.sum(pull, axis=0, keepdims=True))
        here = pl.ds(group * per_group, per_group)
        moves.append(pltpu.make_async_copy(dx_ref.at[:, here], out_ref.at[:, here], sem.at[group]))
        moves[-1].start()
    rows = [jnp.concatenate(row, axis=1) for row in found]
    place_rows(rows, block_ref[1], chan // WIDTH, packet_ref, earlier_ref)
    for move in moves:
        move.wait()


def finish(me_ref, x_ref, gathered_ref, out_ref, alog_out, dskip_out, gain_out, alog_ref, dskip_ref, gain_ref, sem):
    parts, _, share = x_ref.shape
    moves = [
        pltpu.make_async_copy(x_ref.at[i], out_ref.at[0, 0, :, pl.ds(i * share, share)], sem.at[i]) for i in range(parts)
    ]
    for move in moves:
        move.start()
    me = me_ref[0]
    total = sum(gathered_ref[i] for i in range(gathered_ref.shape[0]))
    lanes = gain_ref.shape[2]
    replicas = total.shape[0] // 2
    held = alog_ref.shape[2]
    for block in range(2):
        row = total[block * replicas : block * replicas + 1, 0:lanes]
        skip, log = [total[0:1, lanes + (kind * 2 + block) * replicas * held :] for kind in range(2)]
        skips, logs = skip[:, 0:held], log[:, 0:held]
        for other in range(1, replicas):
            at = block * replicas + other
            row = jnp.where(me == other, total[at : at + 1, 0:lanes], row)
            skips = jnp.where(me == other, skip[:, other * held : (other + 1) * held], skips)
            logs = jnp.where(me == other, log[:, other * held : (other + 1) * held], logs)
        gain_ref[0, block : block + 1] = row
        dskip_ref[0, block : block + 1] = skips
        alog_ref[0, block : block + 1] = logs
    for i, (src, dst) in enumerate(((alog_ref, alog_out), (dskip_ref, dskip_out), (gain_ref, gain_out))):
        moves.append(pltpu.make_async_copy(src, dst, sem.at[parts + i]))
        moves[-1].start()
    for move in moves:
        move.wait()


def relay_out(me_ref, x_ref, out_ref, held_ref, came, gone):
    parts, _, share = out_ref.shape
    ins = [
        pltpu.make_async_copy(x_ref.at[0, 0, :, pl.ds(i * share, share)], held_ref.at[i], came.at[i]) for i in range(parts)
    ]
    places = [place_of(i, me_ref[0] % 2) for i in range(parts)]
    outs = [pltpu.make_async_copy(held_ref.at[i], out_ref.at[places[i]], gone.at[i]) for i in range(parts)]
    for copy in ins:
        copy.start()
    for first, second in zip(ins, outs):
        first.wait()
        second.start()
    for copy in outs:
        copy.wait()


in_vmem = pl.BlockSpec(memory_space=pltpu.VMEM)
in_smem = pl.BlockSpec(memory_space=pltpu.SMEM)
in_any = pl.BlockSpec(memory_space=pl.ANY)
MIB = 1 << 20


def sized(shape, dtype):
    return jax.ShapeDtypeStruct(tuple(shape), dtype)


def call(kernel, name, in_specs, out_specs, out_shape, scratch=(), grant=16, cost=1):
    return pl.pallas_call(
        kernel,
        in_specs=in_specs,
        out_specs=out_specs,
        out_shape=out_shape,
        scratch_shapes=list(scratch),
        compiler_params=pltpu.CompilerParams(vmem_limit_bytes=grant * MIB),
        cost_estimate=pl.CostEstimate(flops=1000, bytes_accessed=cost * 1000 * 1000, transcendentals=0),
        name=name,
    )


def run_forward(tick, block_table, entry_table, x, z, dt, b, c, alog, dskip, gain):
    seq, chan = x.shape[3:]
    groups = b.shape[4]
    heads = dt.shape[3]
    wide = (groups, seq, chan // groups)
    flat = sized((seq, chan), f32)
    outs = [flat, sized((seq, chan), bf16), sized((groups, 3, seq, seq), bf16), sized((2, chan), f32)]
    if tick:
        outs += [flat] * 6
        scratch = [pltpu.VMEM((groups, 2 * seq, chan // groups), f32), pltpu.VMEM((seq, chan), bf16)]
    else:
        outs += [sized((seq, chan), bf16), sized((seq, 3 * heads), f32)]
        scratch = []
    scratch += [
        pltpu.VMEM((seq, chan), bf16),
        pltpu.VMEM(dt.shape[3:], f32),
        pltpu.VMEM(b.shape[3:], bf16),
        pltpu.VMEM(c.shape[3:], bf16),
        pltpu.VMEM((groups, 3 * seq, chan // groups), bf16),
    ]
    scratch += [pltpu.VMEM(wide, f32)] * 5 + [pltpu.SemaphoreType.DMA((5,))]
    in_specs = [in_smem] * 2 + [in_any] * 5 + [in_vmem] * 3
    far = [pltpu.with_memory_space_constraint(a, pltpu.HBM) for a in (x, z, dt, b, c)]
    return call(partial(forward, tick), "forward", in_specs, [in_vmem] * len(outs), outs, scratch, 24, 12)(
        block_table, entry_table, *far, alog, dskip, gain
    )


def backward_scratch(seq, chan, groups):
    wide = (groups, seq, chan // groups)
    tall = (groups, 3 * seq, chan // groups)
    return [pltpu.VMEM(wide, bf16), pltpu.VMEM(tall, bf16)] + [pltpu.VMEM(wide, f32)] * 3 + [pltpu.VMEM(tall, f32)]


def shards(
    grad_in,
    saved_x,
    saved_z,
    saved_dt,
    saved_b,
    saved_c,
    a_log,
    dskip,
    gain,
    block_table,
    entry_table,
):
    parts = lax.axis_size("tensor")
    replicas = lax.axis_size("dp")
    tokens, channels = grad_in.shape[2:]
    share = channels // parts
    seq = tokens * parts
    heads = a_log.shape[2]
    blocks = a_log.shape[1]
    packet = sized((blocks * replicas, share // replicas + LANES), f32)
    block_table = block_table.reshape(-1)
    entry_table = entry_table.reshape(-1)
    steps = jnp.swapaxes(saved_dt, 3, 4)
    me = lax.axis_index("dp").reshape(1)
    staged = call(
        relay_out,
        "relay_out",
        [in_smem, in_any],
        in_any,
        sized((parts, tokens, share), bf16),
        [pltpu.VMEM((parts, tokens, share), bf16)] + [pltpu.SemaphoreType.DMA((parts,))] * 2,
    )(me, pltpu.with_memory_space_constraint(grad_in, pltpu.HBM))
    groups = [[member * replicas + d for member in ORDERS[d % 2]] for d in range(replicas)]
    g = lax.all_to_all(staged, ("tensor", "dp"), split_axis=0, concat_axis=0, axis_index_groups=groups, tiled=True)
    first, last = [
        run_forward(tick, block_table, entry_table, saved_x, saved_z, steps, saved_b, saved_c, a_log, dskip, gain)
        for tick in range(2)
    ]
    scratch = backward_scratch(seq, share, saved_b.shape[4])
    dx = call(backward_first, "backward_first", [in_smem] + [in_vmem] * 7, in_vmem, sized((seq, share), bf16), scratch, 20, 6)(me, g, *first)
    earlier = call(rows_first, "rows_first", [in_smem] * 2 + [in_vmem] * 7, in_vmem, packet, scratch, 20, 6)(
        block_table, me, g, *first
    )
    g = passed_along(dx, "pipe", -1)
    dx, rows = call(
        backward_last,
        "backward_last",
        [in_smem] + [in_vmem] * 12,
        [in_any, in_vmem],
        [pltpu.HBM((seq, share), bf16), packet],
        [pltpu.VMEM((seq, share), bf16), scratch[0], *scratch[2:4], pltpu.SemaphoreType.DMA((saved_b.shape[4],))],
        20,
        6,
    )(block_table, earlier, g, *last)
    out = lax.all_to_all(dx.reshape(parts, tokens, share), "tensor", split_axis=0, concat_axis=0, tiled=True)
    rows = lax.all_gather(rows, "dp")
    shapes = [(1, blocks, heads // replicas)] * 2 + [(1, blocks, share // replicas)]
    out, grad_alog, grad_dskip, grad_gain = call(
        finish,
        "finish",
        [in_smem] + [in_vmem] * 2,
        [in_any] * 4,
        [sized(grad_in.shape, bf16)] + [sized(shape, f32) for shape in shapes],
        [pltpu.VMEM(shape, f32) for shape in shapes] + [pltpu.SemaphoreType.DMA((parts + 3,))],
    )(me, out, rows)
    return (out, grad_alog, grad_dskip, grad_gain)


def solution(mesh):
    placed = (
        P("pipe", "dp", "tensor", None),
        P("pipe", "dp", None, None, "tensor"),
        P("pipe", "dp", None, None, "tensor"),
        P("pipe", "dp", None, None, "tensor"),
        P("pipe", "dp", None, None, "tensor", None),
        P("pipe", "dp", None, None, "tensor", None),
        P("pipe", None, "tensor"),
        P("pipe", None, "tensor"),
        P("pipe", None, "tensor"),
        P(None, "pipe", "dp"),
        P(None, "pipe", "dp"),
    )
    return jax.shard_map(
        shards,
        mesh=mesh,
        in_specs=placed,
        out_specs=(
            P("pipe", "dp", "tensor", None),
            P("pipe", None, ("tensor", "dp")),
            P("pipe", None, ("tensor", "dp")),
            P("pipe", None, ("tensor", "dp")),
        ),
        check_vma=False,
    )
```
